512 devices in a mesh: section: 32 (over z_hi, y, core), tensor: 4 (over z_lo), dp: 4 (over x).
Axes of the slice: x: 4, y: 4, z: 16 (z_hi: 4, z_lo: 4; z = z_hi * 4 + z_lo), core: 2. Of those that a mesh axis runs over, the one named last changes fastest.
Arguments:
- image_rows: bfloat16 [4, 256, 7680], P('dp', 'section'), may hold values from -40 to 40, as said below
- key_weight: bfloat16 [32, 7680, 512], P('section', None, 'tensor'), may hold values from -0.0625 to 0.0625
- value_weight: bfloat16 [32, 7680, 512], P('section', None, 'tensor'), may hold values from -0.0625 to 0.0625
- key_gain: float32 [16, 128], replicated, may hold values from 0.1 to 1.9
- query_gain: float32 [16, 128], replicated, may hold values from 0.1 to 1.9
- queries: bfloat16 [4, 32, 256, 4096], P('dp', 'section', None, 'tensor'), may hold values from -40 to 40, as said below
- cotangent: bfloat16 [4, 32, 256, 4096], P('dp', 'section', None, 'tensor'), may hold values from -6 to 6
- text_doc: int32 [4, 256], P('dp'), may hold values from 0 to 7, never falling along the last dimension, each value on 1 to 128 neighbouring positions
- row_doc: int32 [4, 256], P('dp'), may hold values from 0 to 7, never falling along the last dimension, each value on 1 to 128 neighbouring positions
Outputs:
- grad_rows: bfloat16 [4, 256, 7680], P('dp', 'section', 'tensor')
- key_gain_grad: float32 [32, 128], P('section')
- query_gain_grad: float32 [32, 128], P('section')
The draws below stay inside these ranges and needn't reach their ends.
Inputs may be any that keep to these rules, and one draw needn't show every extreme that they name: `image_rows`: real values of order one. `queries`: real values of order one.
All inputs are finite; a program needn't handle non-finite values.
Results may differ from the reference program's by a relative error of at most 0.024.
Values may be sent and summed in bfloat16 or wider, within the bound.
A program may use at most 64 MiB of HBM per device.

```python
import math
import jax
import jax.numpy as jnp
import numpy as np
from jax import lax

VW = 7680
HEAD = 128
TOK = 256
NDOC = 8
KV_HALF = 4
Q_HALF = 32
REPL = 4
SECTIONS = 32
LAYERS = 16
IMG = 256


def spread_scale(key, shape):
    return jnp.exp(jax.random.uniform(key, shape, jnp.float32, math.log(0.3), math.log(3.0)))


def draw_image_rows(key, part):
    key = jax.random.fold_in(key, 5)
    keys = jax.random.split(key, 3)
    shape = (REPL, IMG, VW)
    row_scale = spread_scale(keys[0], (REPL, IMG, 1))
    column_scale = spread_scale(keys[1], (VW,))
    base = jax.random.truncated_normal(keys[2], -4.0, 4.0, shape, jnp.float32)
    return (base * row_scale * column_scale).astype(jnp.bfloat16)


def draw_queries(key, part):
    key = jax.random.fold_in(key, 7)
    keys = jax.random.split(key, 3)
    shape = (REPL, SECTIONS, TOK, Q_HALF * HEAD)
    row_scale = spread_scale(keys[0], (REPL, SECTIONS, TOK, 1))
    column_scale = spread_scale(keys[1], (Q_HALF * HEAD,))
    base = jax.random.truncated_normal(keys[2], -4.0, 4.0, shape, jnp.float32)
    return (base * row_scale * column_scale).astype(jnp.bfloat16)


def level_of(stream_key, shape, cuts, low, high):
    def one(dim, parts):
        draws = jax.random.uniform(jax.random.fold_in(jax.random.fold_in(stream_key, 6), dim), (parts,), jnp.float32, low / len(cuts), high / len(cuts))
        return jnp.repeat(jnp.exp(draws), shape[dim] // parts).reshape((-1,) + (1,) * (len(shape) - dim - 1))

    level = one(*cuts[0])
    for cut in cuts[1:]:
        level = level * one(*cut)
    return level


def profile(amount, total, bound, skew):
    portions = [(1 << 20) // math.isqrt(rank ** skew) + 1 for rank in range(2, amount + 1)]
    rest, given = total - bound - (amount - 1), [1] * (amount - 1)
    while rest > 0:
        candidates = [i for i in range(amount - 1) if given[i] < bound]
        pool, remaining = sum([portions[i] for i in candidates]), rest
        for i in candidates:
            addition = min(bound - given[i], max(1, remaining * portions[i] // pool), rest)
            given[i] = given[i] + addition
            rest = rest - addition
    return np.array([bound] + given)


def ragged_sizes(rng, amount, total, reach, skew):
    if amount == 2:
        one = jax.random.randint(rng, (), max(1, total - reach), min(reach, total - 1) + 1)
        return jnp.stack([one, total - one])
    sizes = jnp.asarray(profile(amount, total, reach, skew), jnp.int32)
    twos = (amount - 1) // 2
    donor, taker = sizes[1:1 + 2 * twos:2], sizes[2:2 + 2 * twos:2]
    slack = jnp.minimum(donor - 1, reach - taker)
    passed = jax.random.randint(jax.random.fold_in(rng, 1), (twos,), 0, 1 << 20) % (slack + 1)
    sizes = sizes.at[1:1 + 2 * twos:2].set(donor - passed).at[2:2 + 2 * twos:2].set(taker + passed)
    return sizes[jax.random.permutation(jax.random.fold_in(rng, 2), amount)]


def normal_values(key, shape, spread, bound, pieces=(), dtype=jnp.bfloat16):
    result = jax.random.normal(key, shape, jnp.float32) * spread
    if len(pieces) > 0:
        result = level_of(key, shape, pieces, -0.22, 0.18) * result
    return jnp.clip(result, min=-bound, max=bound).astype(dtype)


def setup_inputs(seed: int = 0) -> dict:
    streams_of = jax.random.split(jax.random.key(seed), 10)
    return {
        "image_rows": draw_image_rows(jax.random.fold_in(streams_of[9], 71), 0),
        "key_weight": normal_values(streams_of[1], (SECTIONS, VW, KV_HALF * HEAD), VW ** -0.5, 0.0625, ((0, 32), (2, 4))),
        "value_weight": normal_values(streams_of[2], (SECTIONS, VW, KV_HALF * HEAD), VW ** -0.5, 0.0625, ((0, 32), (2, 4))),
        "key_gain": jnp.clip(1.0 + 0.18 * jax.random.normal(streams_of[3], (LAYERS, HEAD), jnp.float32), 0.1, 1.9),
        "query_gain": jnp.clip(1.0 + 0.18 * jax.random.normal(streams_of[4], (LAYERS, HEAD), jnp.float32), 0.1, 1.9),
        "queries": draw_queries(jax.random.fold_in(streams_of[9], 71), 0),
        "cotangent": normal_values(streams_of[6], (REPL, SECTIONS, TOK, Q_HALF * HEAD), 1.0, 6.0, ((0, 4), (1, 32), (3, 4))),
        "text_doc": jax.vmap(lambda own: jnp.searchsorted(jnp.cumsum(ragged_sizes(own, NDOC, TOK, TOK // 2, 1)), jnp.arange(TOK), side="right"))(jax.random.split(streams_of[7], REPL)).reshape((REPL, TOK)).astype(jnp.int32),
        "row_doc": jax.vmap(lambda own: jnp.searchsorted(jnp.cumsum(ragged_sizes(own, NDOC, IMG, IMG // 2, 1)), jnp.arange(IMG), side="right"))(jax.random.split(streams_of[8], REPL)).reshape((REPL, IMG)).astype(jnp.int32),
    }


EPSILON = 1e-05

def head_norm(inputs_raw, scaling):
    inverse_rms = lax.rsqrt(lax.optimization_barrier(jnp.mean(inputs_raw * inputs_raw, axis=-1, keepdims=True)) + EPSILON)
    normalized = inputs_raw * inverse_rms
    return (normalized, inverse_rms, normalized * scaling)

def norm_back(upstream, normalized, inverse_rms, scaling):
    scaled_up = upstream * scaling
    return inverse_rms * (scaled_up - normalized * lax.optimization_barrier(jnp.mean(scaled_up * normalized, axis=-1, keepdims=True)))

def attend_back(queries_in, keys_in, values_in, upstream, allowed):
    tok_rows, query_heads, head_size = queries_in.shape
    key_heads = keys_in.shape[1]
    group_size = query_heads // key_heads
    factor = 1.0 / math.sqrt(head_size)
    query_wide = queries_in.astype(jnp.float32).reshape(tok_rows, key_heads, group_size, head_size)
    upstream_wide = upstream.astype(jnp.float32).reshape(tok_rows, key_heads, group_size, head_size)
    key_wide = keys_in.astype(jnp.float32)
    value_wide = values_in.astype(jnp.float32)
    scores = jnp.einsum('ikgd,jkd->kgij', query_wide, key_wide) * factor
    exponents = jnp.where(allowed[None, None], jnp.exp(scores), 0.0)
    softmax = exponents / lax.optimization_barrier(jnp.sum(exponents, axis=-1, keepdims=True))
    rounded = softmax.astype(jnp.bfloat16)
    grad_softmax = jnp.einsum('ikgd,jkd->kgij', upstream_wide, value_wide)
    inner_sum = lax.optimization_barrier(jnp.sum(softmax * grad_softmax, axis=-1, keepdims=True))
    grad_scores = (softmax * (grad_softmax - inner_sum)).astype(jnp.bfloat16)
    grad_value = jnp.einsum('kgij,ikgd->jkd', rounded.astype(jnp.float32), upstream_wide).astype(jnp.bfloat16)
    grad_key = jnp.einsum('kgij,ikgd->jkd', grad_scores.astype(jnp.float32), query_wide) * factor
    grad_query = jnp.einsum('kgij,jkd->ikgd', grad_scores.astype(jnp.float32), key_wide) * factor
    return (grad_query.reshape(tok_rows, query_heads, head_size), grad_key, grad_value)

def reference(image_rows, key_weight, value_weight, key_gain, query_gain, queries, cotangent, text_doc, row_doc):
    results = []
    key_total = jnp.zeros((SECTIONS, HEAD), jnp.float32)
    query_total = jnp.zeros((SECTIONS, HEAD), jnp.float32)
    key_gains = jnp.repeat(key_gain, 2, axis=0)
    query_gains = jnp.repeat(query_gain, 2, axis=0)
    for replica in range(REPL):
        image_block = image_rows[replica]
        allowed = text_doc[replica][:, None] == row_doc[replica][None, :]

        def section_step(running, section_data):
            key_matrix, value_matrix, key_scaling, query_scaling, query_raw, upstream = section_data
            key_raw = jnp.dot(image_block, key_matrix, preferred_element_type=jnp.float32).reshape(IMG, KV_HALF, HEAD)
            values_all = jnp.dot(image_block, value_matrix, preferred_element_type=jnp.float32).astype(jnp.bfloat16).reshape(IMG, KV_HALF, HEAD)
            key_normed, key_scale, key_scaled = head_norm(key_raw, key_scaling)
            query_normed, query_scale, query_scaled = head_norm(query_raw.astype(jnp.float32).reshape(TOK, Q_HALF, HEAD), query_scaling)
            grad_query, grad_key, grad_value = attend_back(query_scaled.astype(jnp.bfloat16), key_scaled.astype(jnp.bfloat16), values_all, upstream.reshape(TOK, Q_HALF, HEAD), allowed)
            gain_key = lax.optimization_barrier(jnp.sum(grad_key * key_normed, axis=(0, 1)))
            gain_query = lax.optimization_barrier(jnp.sum(grad_query * query_normed, axis=(0, 1)))
            key_back = norm_back(grad_key, key_normed, key_scale, key_scaling).astype(jnp.bfloat16)
            key_terms = jnp.einsum('jkc,vkc->kjv', key_back.astype(jnp.float32), key_matrix.astype(jnp.float32).reshape(VW, KV_HALF, HEAD))
            value_terms = jnp.einsum('jkc,vkc->kjv', grad_value.astype(jnp.float32), value_matrix.astype(jnp.float32).reshape(VW, KV_HALF, HEAD))
            row_terms = lax.optimization_barrier((key_terms + value_terms).astype(jnp.bfloat16)).astype(jnp.float32)
            return (running + lax.optimization_barrier(jnp.sum(row_terms, axis=0)), (gain_key, gain_query))
        summed, gains = lax.scan(section_step, jnp.zeros((IMG, VW), jnp.float32), (key_weight, value_weight, key_gains, query_gains, queries[replica], cotangent[replica]))
        results.append(summed.astype(jnp.bfloat16))
        key_total = key_total + gains[0]
        query_total = query_total + gains[1]
    return (jnp.stack(results), key_total, query_total)
```

```python
import math

import jax
import jax.numpy as jnp
from jax import lax
from jax.experimental import pallas as pl
from jax.experimental.pallas import tpu as pltpu
from jax.sharding import PartitionSpec as P

HEAD = 128
EPSILON = 1e-05
MESH = pl.DeviceIdType.MESH
F32 = jnp.float32
BF16 = jnp.bfloat16
ROWS = 16


def kernel(
    x_ref, kw_ref, vw_ref, kg_ref, qg_ref, q_hbm, ct_hbm, td_ref, rd_ref,
    out_ref, gk_out, gq_out,
    wb, q_buf, ct_buf, qs_buf, qn_buf, xs, xr, g, raw, raw_send, raw_recv, kv, p,
    y1, y2, ysum, yred, zin, zred, zf, fs, fr, gain_a, gain_b, mask,
    w_sem, w_ss, w_rs, qc_sem, x_ss, x_rs, zo_ss, zf_ss, z_rs, ys_ss, y_rs, yf_ss, yf_rs,
    pr_ss, pr_rs, kv_ss, kv_rs, r1_ss, r1_rs, r2_ss, r2_rs, r3_ss, r3_rs,
    in_ss, in_rs, z4_ss, z4_rs, f_ss, f_rs, ga_ss, ga_rs, gb_ss, gb_rs,
):
    s = lax.axis_index("section")
    l = lax.axis_index("tensor")
    xi = lax.axis_index("dp")
    a = s // 8
    y = (s // 2) % 4
    c = s % 2
    half = g.shape[1]
    quarter = half // 2
    tok = q_buf.shape[0]
    heads = q_buf.shape[1] // HEAD
    rows = g.shape[0]
    block = 4 * ROWS
    layer = s // 2

    def dev(a_=None, y_=None, c_=None, l_=None, x_=None):
        a_ = a if a_ is None else lax.rem(a_ + 8, 4)
        y_ = y if y_ is None else lax.rem(y_ + 8, 4)
        c_ = c if c_ is None else c_
        return {
            "section": (a_ * 4 + y_) * 2 + c_,
            "tensor": l if l_ is None else l_,
            "dp": xi if x_ is None else x_,
        }

    def remote(src, dst, ss, rs, to):
        return pltpu.make_async_remote_copy(
            src_ref=src, dst_ref=dst, send_sem=ss, recv_sem=rs, device_id=to, device_id_type=MESH
        )

    partner = dev(c_=1 - c)
    edge = jnp.logical_or(l == 0, l == 3)
    even = lax.rem(l, 2) == 0
    mate = jnp.where(even, l + 1, l - 1)
    step = jnp.where(even, 1, -1)
    a_of = [a, lax.rem(a - step + 4, 4), lax.rem(a + step + 4, 4), lax.rem(a + 2, 4)]

    barrier = pltpu.get_barrier_semaphore()

    def greet(to):
        pl.semaphore_signal(barrier, inc=1, device_id=to, device_id_type=MESH)

    greet(partner)
    greet(dev(y_=y + 1))
    greet(dev(y_=y - 1))
    for d in range(1, 4):
        greet(dev(l_=lax.rem(l + d, 4)))
        greet(dev(a_=a + d))
        greet(dev(x_=lax.rem(xi + d, 4)))

    greet(dev(a_=a - step, l_=jnp.where(even, 3, 0)))

    @pl.when(edge)
    def _():
        greet(dev(a_=a + 2, l_=jnp.where(l == 0, 3, 0)))

    own_rows = pl.ds(pl.multiple_of(c * half, 128), half)
    their_rows = pl.ds(pl.multiple_of((1 - c) * half, 128), half)
    loads = [
        pltpu.make_async_copy(kw_ref.at[own_rows, :], wb.at[:, 0:HEAD], w_sem.at[0]),
        pltpu.make_async_copy(vw_ref.at[own_rows, :], wb.at[:, HEAD : 2 * HEAD], w_sem.at[1]),
        pltpu.make_async_copy(q_hbm, q_buf, qc_sem.at[0]),
        pltpu.make_async_copy(ct_hbm, ct_buf, qc_sem.at[1]),
    ]
    for copy in loads:
        copy.start()
    low = x_ref[:, :half].astype(F32)
    high = x_ref[:, half:].astype(F32)
    first = c == 0
    own = jnp.where(first, low, high)
    xs[...] = jnp.where(first, high, low)
    pl.semaphore_wait(barrier, 12 + jnp.where(edge, 3, 0))

    pending = []

    def send(copy, when=None):
        pending.append((when, copy))
        if when is None:
            copy.start()
        else:
            pl.when(when)(copy.start)

    send(remote(xs, xr, x_ss, x_rs, partner))
    x_copy = pending[-1][1]
    x_copy.wait_recv()
    got = xr[...]
    mine = pl.ds(pl.multiple_of((a * 4 + y) * ROWS, ROWS), ROWS)
    g[mine, :] = jnp.concatenate(
        [jnp.where(first, own, got), jnp.where(first, got, own)], axis=0
    ).astype(BF16)

    def shard(a_, y_, h):
        y_ = lax.rem(y_ + 8, 4)
        at = pl.ds(pl.multiple_of((a_ * 4 + y_) * ROWS, ROWS), ROWS)
        return g.at[at, h * quarter : (h + 1) * quarter]

    def y_send(k, h):
        piece = shard(a_of[k], y, h)
        send(remote(piece, piece, ys_ss.at[k, h, 0], y_rs.at[k, h, 0], dev(y_=y + 1)))
        send(remote(piece, piece, ys_ss.at[k, h, 1], y_rs.at[k, h, 1], dev(y_=y - 1)))

    def y_wait(k, h, side):
        piece = shard(a_of[k], y - 1 if side == 0 else y + 1, h)
        remote(piece, piece, ys_ss.at[k, h, side], y_rs.at[k, h, side], partner).wait_recv()

    def y_forward(k):
        for side in range(2):
            y_wait(k, side, side)
            piece = shard(a_of[k], y - 1 if side == 0 else y + 1, side)
            to = dev(y_=y + 1 if side == 0 else y - 1)
            send(remote(piece, piece, yf_ss.at[k, side], yf_rs.at[k, side], to))

    def y_finish(k):
        for side in range(2):
            y_wait(k, 1 - side, side)
        for side in range(2):
            piece = shard(a_of[k], y + 2, side)
            remote(piece, piece, yf_ss.at[k, side], yf_rs.at[k, side], partner).wait_recv()

    def z_wait(k, h):
        piece = shard(a_of[k], y, h)
        remote(piece, piece, zf_ss.at[0, h], z_rs.at[k, h], partner).wait_recv()

    last = l == 3
    far = jnp.where(last, 0, 3)
    side_a = jnp.where(last, a + 1, a - 1)
    targets = [
        (dev(a_=side_a, l_=far), 1),
        (dev(a_=side_a, l_=jnp.where(last, 2, 1)), 1),
        (dev(a_=a + 2, l_=far), 3),
    ]
    for h in range(2):
        piece = shard(a, y, h)
        to, k = targets[0]
        send(remote(piece, piece, zo_ss.at[0, h], z_rs.at[k, h], to), edge)
        y_send(0, h)
    for i in range(1, 3):
        for h in range(2):
            piece = shard(a, y, h)
            to, k = targets[i]
            send(remote(piece, piece, zo_ss.at[i, h], z_rs.at[k, h], to), edge)
    send(remote(kw_ref.at[their_rows, :], wb.at[:, 2 * HEAD : 3 * HEAD], w_ss.at[0], w_rs.at[0], partner))
    send(remote(vw_ref.at[their_rows, :], wb.at[:, 3 * HEAD : 4 * HEAD], w_ss.at[1], w_rs.at[1], partner))
    w_copies = [pending[-2][1], pending[-1][1]]

    loads[2].wait()
    q_gain = qg_ref[pl.ds(layer, 1), :]
    k_gain = kg_ref[pl.ds(layer, 1), :]

    def norm_queries(h, carry):
        at = pl.ds(pl.multiple_of(h * HEAD, HEAD), HEAD)
        raw_q = q_buf[:, at].astype(F32)
        scale = lax.rsqrt(jnp.mean(raw_q * raw_q, axis=-1, keepdims=True) + EPSILON)
        normed = raw_q * scale
        qn_buf[:, at] = normed
        qs_buf[:, at] = (normed * q_gain).astype(BF16)
        return carry

    lax.fori_loop(0, heads, norm_queries, 0)
    row_doc = jnp.broadcast_to(rd_ref[...].astype(F32), (rows, rows)).T
    mask[...] = jnp.where(row_doc == td_ref[...].astype(F32), 1.0, 0.0)

    y_forward(0)
    for h in range(2):
        z_wait(1, h)
        piece = shard(a_of[1], y, h)
        send(remote(piece, piece, zf_ss.at[0, h], z_rs.at[2, h], dev(l_=mate)))
        y_send(1, h)

    def project(k):
        y_finish(k)
        at = pl.ds(pl.multiple_of(a_of[k] * block, block), block)
        out = jnp.dot(g[at, :], wb[...], preferred_element_type=F32)
        raw[at, :] = out[:, : 2 * HEAD]
        raw_send[at, :] = out[:, 2 * HEAD :]
        send(remote(raw_send.at[at, :], raw_recv.at[at, :], pr_ss.at[k], pr_rs.at[k], partner))

    loads[0].wait()
    loads[1].wait()
    for copy in w_copies:
        copy.wait_recv()
    loads[3].wait()
    project(0)
    for h in range(2):
        z_wait(2, h)
        y_send(2, h)
    y_forward(1)
    for h in range(2):
        z_wait(3, h)
        piece = shard(a_of[3], y, h)
        send(remote(piece, piece, zf_ss.at[1, h], z_rs.at[3, h], dev(l_=mate)), edge)
        y_send(3, h)
    y_forward(2)
    project(1)
    y_forward(3)
    project(2)
    project(3)

    for k in range(4):
        at = pl.ds(pl.multiple_of(a_of[k] * block, block), block)
        remote(raw_send.at[at, :], raw_recv.at[at, :], pr_ss.at[k], pr_rs.at[k], partner).wait_recv()
    projected = raw[...] + raw_recv[...]
    key_raw = projected[:, :HEAD]
    values = projected[:, HEAD:].astype(BF16)
    key_scale = lax.rsqrt(jnp.mean(key_raw * key_raw, axis=-1, keepdims=True) + EPSILON)
    key_normed = key_raw * key_scale
    keys = (key_normed * k_gain).astype(BF16)
    factor = 1.0 / math.sqrt(HEAD)
    nt = (((1,), (1,)), ((), ()))
    tn = (((0,), (0,)), ((), ()))

    def head(h, carry):
        grad_key, grad_value, gain = carry
        at = pl.ds(pl.multiple_of(h * HEAD, HEAD), HEAD)
        query = qs_buf[:, at]
        upstream = ct_buf[:, at]
        scores = lax.dot_general(keys, query, nt, preferred_element_type=F32) * factor
        exponents = jnp.exp(scores) * mask[...]
        softmax = exponents * (1.0 / jnp.sum(exponents, axis=0, keepdims=True))
        grad_softmax = lax.dot_general(values, upstream, nt, preferred_element_type=F32)
        inner = jnp.sum(softmax * grad_softmax, axis=0, keepdims=True)
        grad_scores = (softmax * (grad_softmax - inner)).astype(BF16)
        grad_value = grad_value + jnp.dot(softmax.astype(BF16), upstream, preferred_element_type=F32)
        grad_key = grad_key + jnp.dot(grad_scores, query, preferred_element_type=F32)
        grad_query = lax.dot_general(grad_scores, keys, tn, preferred_element_type=F32)
        gain = gain + jnp.sum(grad_query * qn_buf[:, at], axis=0, keepdims=True)
        return grad_key, grad_value, gain

    zero = jnp.zeros((rows, HEAD), F32)
    grad_key, grad_value, gain_query = lax.fori_loop(
        0, heads, head, (zero, zero, jnp.zeros((1, HEAD), F32))
    )
    grad_key = grad_key * factor
    scaled_up = grad_key * k_gain
    key_back = key_scale * (
        scaled_up - key_normed * jnp.mean(scaled_up * key_normed, axis=-1, keepdims=True)
    )
    kv[:, :HEAD] = key_back.astype(BF16)
    kv[:, HEAD : 2 * HEAD] = grad_value.astype(BF16)
    kv_copy = remote(kv.at[:, : 2 * HEAD], kv.at[:, 2 * HEAD :], kv_ss, kv_rs, partner)
    send(kv_copy)

    gain_a[l] = jnp.concatenate(
        [
            jnp.sum(grad_key * key_normed, axis=0, keepdims=True),
            gain_query * factor,
            jnp.zeros((6, HEAD), F32),
        ],
        axis=0,
    )
    for d in range(1, 4):
        to = dev(l_=lax.rem(l + d, 4))
        send(remote(gain_a.at[l], gain_a.at[l], ga_ss.at[d - 1], ga_rs.at[d - 1], to))
    kv_copy.wait_recv()

    b_of = [lax.rem(a + 2, 4), lax.rem(a + 1, 4), lax.rem(a + 3, 4), a]
    y_up, y_down = dev(y_=y + 1), dev(y_=y - 1)

    def part(b, y_, h):
        y_ = lax.rem(y_ + 8, 4)
        at = pl.ds(pl.multiple_of((b * 4 + y_) * ROWS, ROWS), ROWS)
        return p.at[at, h * quarter : (h + 1) * quarter]

    def terms(k):
        b = b_of[k]
        at = pl.ds(pl.multiple_of(b * block, block), block)
        left = kv[at, :]
        for h in range(2):
            cols = slice(h * quarter, (h + 1) * quarter)
            p[at, cols] = lax.dot_general(
                left, wb[cols, :], nt, preferred_element_type=F32
            ).astype(BF16)
            send(remote(part(b, y + 2, h), y1.at[h, k], r1_ss.at[h, k], r1_rs.at[h, k], y_up if h == 0 else y_down))
        for h in range(2):
            src = part(b, y + 1, 1) if h == 0 else part(b, y - 1, 0)
            dst = y2.at[h, k, 1 - h]
            send(remote(src, dst, r2_ss.at[h, k], r2_rs.at[h, k], y_up if h == 0 else y_down))

    def pass_on(k):
        b = b_of[k]
        for h in range(2):
            remote(y1.at[h, k], y1.at[h, k], r1_ss.at[h, k], r1_rs.at[h, k], partner).wait_recv()
            mine_ = part(b, y + 1, 0) if h == 0 else part(b, y - 1, 1)
            ysum[h, k] = (mine_[...].astype(F32) + y1[h, k].astype(F32)).astype(BF16)
            send(remote(ysum.at[h, k], y2.at[h, k, h], r3_ss.at[h, k], r3_rs.at[h, k], y_up if h == 0 else y_down))

    active = c == l // 2

    def group(k):
        b = b_of[k]
        for h in range(2):
            remote(y2.at[h, k, 1 - h], y2.at[h, k, 1 - h], r2_ss.at[h, k], r2_rs.at[h, k], partner).wait_recv()
            remote(y2.at[h, k, h], y2.at[h, k, h], r3_ss.at[h, k], r3_rs.at[h, k], partner).wait_recv()
        for i in range(2):
            yred[k, i] = (
                part(b, y, i)[...].astype(F32) + y2[0, k, i].astype(F32) + y2[1, k, i].astype(F32)
            ).astype(BF16)
            to = 2 * c + i
            slot = lax.rem(l - to + 4, 4)
            slot_ = jnp.maximum(slot - 1, 0)
            send(
                remote(yred.at[k, i], zin.at[k, slot_], in_ss.at[k, i], in_rs.at[k, slot_], dev(l_=to)),
                to != l,
            )

    def group_sum(k):
        for d in range(3):
            remote(zin.at[k, d], zin.at[k, d], in_ss.at[k, 0], in_rs.at[k, d], partner).wait_recv()
        total = jnp.where(even, yred[k, 0].astype(F32), yred[k, 1].astype(F32))
        for d in range(3):
            total = total + zin[k, d].astype(F32)
        return total

    def across(k):
        @pl.when(active)
        def _():
            zred[k] = group_sum(k).astype(BF16)
            z4_copy(k).start()

    def z4_copy(k):
        return remote(zred.at[k], zf.at[k], z4_ss.at[k], z4_rs.at[k], dev(a_=b_of[k]))

    terms(0)
    terms(1)
    pass_on(0)
    terms(2)
    pass_on(1)
    terms(3)

    for d in range(1, 4):
        src = gain_a.at[lax.rem(l - d + 4, 4)]
        remote(src, src, ga_ss.at[d - 1], ga_rs.at[d - 1], partner).wait_recv()
    gain_b[xi] = gain_a[0] + gain_a[1] + gain_a[2] + gain_a[3]
    for d in range(1, 4):
        to = dev(x_=lax.rem(xi + d, 4))
        send(remote(gain_b.at[xi], gain_b.at[xi], gb_ss.at[d - 1], gb_rs.at[d - 1], to))

    group(0)
    pass_on(2)
    group(1)
    across(0)
    pass_on(3)
    group(2)
    across(1)
    group(3)
    across(2)

    for d in range(1, 4):
        src = gain_b.at[lax.rem(xi - d + 4, 4)]
        remote(src, src, gb_ss.at[d - 1], gb_rs.at[d - 1], partner).wait_recv()
    gains = gain_b[0] + gain_b[1] + gain_b[2] + gain_b[3]
    gk_out[...] = gains[0:1]
    gq_out[...] = gains[1:2]

    f_copy = remote(fs, fr, f_ss, f_rs, partner)

    @pl.when(active)
    def _():
        total = group_sum(3)
        for k in range(3):
            z4_copy(k).wait_recv()
            total = total + zf[k].astype(F32)
        top, bottom = total[: ROWS // 2], total[ROWS // 2 :]
        fs[...] = jnp.where(first, bottom, top)
        f_copy.start()
        out_ref[...] = jnp.where(first, top, bottom).astype(BF16)
        for k in range(3):
            z4_copy(k).wait_send()
        f_copy.wait_send()

    @pl.when(jnp.logical_not(active))
    def _():
        f_copy.wait_recv()
        out_ref[...] = fr[...].astype(BF16)

    for when, copy in pending:
        if when is None:
            copy.wait_send()
        else:
            pl.when(when)(copy.wait_send)


def on_device(
    image_rows,
    key_weight,
    value_weight,
    key_gain,
    query_gain,
    queries,
    cotangent,
    text_doc,
    row_doc,
):
    width = image_rows.shape[2]
    half = width // 2
    quarter = half // 2
    tok = queries.shape[2]
    q_width = queries.shape[3]
    rows = row_doc.shape[1]
    vmem = pl.BlockSpec(memory_space=pltpu.VMEM)
    anywhere = pl.BlockSpec(memory_space=pl.ANY)
    dma = pltpu.SemaphoreType.DMA
    scratch = [
        pltpu.VMEM((half, 4 * HEAD), BF16),
        pltpu.VMEM((tok, q_width), BF16),
        pltpu.VMEM((tok, q_width), BF16),
        pltpu.VMEM((tok, q_width), BF16),
        pltpu.VMEM((tok, q_width), F32),
        pltpu.VMEM((8, half), F32),
        pltpu.VMEM((8, half), F32),
        pltpu.VMEM((rows, half), BF16),
        pltpu.VMEM((rows, 2 * HEAD), F32),
        pltpu.VMEM((rows, 2 * HEAD), F32),
        pltpu.VMEM((rows, 2 * HEAD), F32),
        pltpu.VMEM((rows, 4 * HEAD), BF16),
        pltpu.VMEM((rows, half), BF16),
        pltpu.VMEM((2, 4, ROWS, quarter), BF16),
        pltpu.VMEM((2, 4, 2, ROWS, quarter), BF16),
        pltpu.VMEM((2, 4, ROWS, quarter), BF16),
        pltpu.VMEM((4, 2, ROWS, quarter), BF16),
        pltpu.VMEM((4, 3, ROWS, quarter), BF16),
        pltpu.VMEM((3, ROWS, quarter), BF16),
        pltpu.VMEM((3, ROWS, quarter), BF16),
        pltpu.VMEM((8, quarter), F32),
        pltpu.VMEM((8, quarter), F32),
        pltpu.VMEM((4, 8, HEAD), F32),
        pltpu.VMEM((4, 8, HEAD), F32),
        pltpu.VMEM((rows, tok), F32),
        dma((2,)), dma((2,)), dma((2,)), dma((2,)), dma, dma,
        dma((3, 2)), dma((2, 2)), dma((4, 2)),
        dma((4, 2, 2)), dma((4, 2, 2)), dma((4, 2)), dma((4, 2)),
        dma((4,)), dma((4,)), dma, dma,
        dma((2, 4)), dma((2, 4)), dma((2, 4)), dma((2, 4)), dma((2, 4)), dma((2, 4)),
        dma((4, 2)), dma((4, 3)), dma((3,)), dma((3,)), dma, dma,
        dma((3,)), dma((3,)), dma((3,)), dma((3,)),
    ]
    grad, gain_key, gain_query = pl.pallas_call(
        kernel,
        name="image_row_gradients",
        out_shape=(
            jax.ShapeDtypeStruct((8, quarter), BF16),
            jax.ShapeDtypeStruct((1, HEAD), F32),
            jax.ShapeDtypeStruct((1, HEAD), F32),
        ),
        in_specs=[vmem, anywhere, anywhere, vmem, vmem, anywhere, anywhere, vmem, vmem],
        out_specs=(vmem, vmem, vmem),
        scratch_shapes=scratch,
        compiler_params=pltpu.CompilerParams(
            collective_id=0, has_side_effects=True, vmem_limit_bytes=48 * 1024 * 1024
        ),
    )(
        image_rows[0], key_weight[0], value_weight[0], key_gain, query_gain,
        queries[0, 0], cotangent[0, 0], text_doc, row_doc,
    )
    return (grad[None], gain_key, gain_query)


def solution(mesh):
    in_specs = (
        P("dp", "section", None),
        P("section", None, "tensor"),
        P("section", None, "tensor"),
        P(),
        P(),
        P("dp", "section", None, "tensor"),
        P("dp", "section", None, "tensor"),
        P("dp", None),
        P("dp", None),
    )
    out_specs = (P("dp", "section", "tensor"), P("section", None), P("section", None))
    return jax.shard_map(
        on_device, mesh=mesh, in_specs=in_specs, out_specs=out_specs, check_vma=False
    )
```

```python
import math

import jax
import jax.numpy as jnp
from jax import lax
from jax.experimental import pallas as pl
from jax.experimental.pallas import tpu as pltpu
from jax.sharding import PartitionSpec as P

HEAD = 128
EPSILON = 1e-05
MESH = pl.DeviceIdType.MESH
F32 = jnp.float32
BF16 = jnp.bfloat16
ROWS = 16


def kernel(
    x_hbm, kw_ref, vw_ref, kg_hbm, qg_hbm, q_hbm, ct_hbm, td_hbm, rd_hbm,
    out_ref, gk_out, gq_out,
    x_ref, kg_ref, qg_ref, td_ref, rd_ref,
    wb, q_buf, ct_buf, qs_buf, qn_buf, xs, xr, g, raw, raw_send, raw_recv, kv, p,
    y1, y2, ysum, yred, zin, zred, zf, fs, fr, gain_a, gain_b, mask,
    s_sem, w_sem, w_ss, w_rs, qc_sem, x_ss, x_rs, zo_ss, zf_ss, z_rs, ys_ss, y_rs, yf_ss, yf_rs,
    pr_ss, pr_rs, kv_ss, kv_rs, r1_ss, r1_rs, r2_ss, r2_rs, r3_ss, r3_rs,
    in_ss, in_rs, z4_ss, z4_rs, f_ss, f_rs, ga_ss, ga_rs, gb_ss, gb_rs,
):
    s = lax.axis_index("section")
    l = lax.axis_index("tensor")
    xi = lax.axis_index("dp")
    a = s // 8
    y = (s // 2) % 4
    c = s % 2
    half = g.shape[1]
    quarter = half // 2
    tok = q_buf.shape[0]
    heads = q_buf.shape[1] // HEAD
    rows = g.shape[0]
    block = 4 * ROWS
    layer = s // 2

    def dev(a_=None, y_=None, c_=None, l_=None, x_=None):
        a_ = a if a_ is None else lax.rem(a_ + 8, 4)
        y_ = y if y_ is None else lax.rem(y_ + 8, 4)
        c_ = c if c_ is None else c_
        return {
            "section": (a_ * 4 + y_) * 2 + c_,
            "tensor": l if l_ is None else l_,
            "dp": xi if x_ is None else x_,
        }

    def remote(src, dst, ss, rs, to):
        return pltpu.make_async_remote_copy(
            src_ref=src, dst_ref=dst, send_sem=ss, recv_sem=rs, device_id=to, device_id_type=MESH
        )

    partner = dev(c_=1 - c)
    edge = jnp.logical_or(l == 0, l == 3)
    even = lax.rem(l, 2) == 0
    mate = jnp.where(even, l + 1, l - 1)
    step = jnp.where(even, 1, -1)
    a_of = [a, lax.rem(a - step + 4, 4), lax.rem(a + step + 4, 4), lax.rem(a + 2, 4)]

    small = [
        pltpu.make_async_copy(src, dst, s_sem.at[i])
        for i, (src, dst) in enumerate(
            [(x_hbm, x_ref), (kg_hbm, kg_ref), (qg_hbm, qg_ref), (td_hbm, td_ref), (rd_hbm, rd_ref)]
        )
    ]
    for copy in small:
        copy.start()

    barrier = pltpu.get_barrier_semaphore()

    def greet(to):
        pl.semaphore_signal(barrier, inc=1, device_id=to, device_id_type=MESH)

    greet(partner)
    greet(dev(y_=y + 1))
    greet(dev(y_=y - 1))
    for d in range(1, 4):
        greet(dev(l_=lax.rem(l + d, 4)))
        greet(dev(x_=lax.rem(xi + d, 4)))

    greet(dev(a_=a - step, l_=jnp.where(even, 3, 0)))

    own_rows = pl.ds(pl.multiple_of(c * half, 128), half)
    their_rows = pl.ds(pl.multiple_of((1 - c) * half, 128), half)
    loads = [
        pltpu.make_async_copy(kw_ref.at[own_rows, :], wb.at[:, 0:HEAD], w_sem.at[0]),
        pltpu.make_async_copy(vw_ref.at[own_rows, :], wb.at[:, HEAD : 2 * HEAD], w_sem.at[1]),
        pltpu.make_async_copy(q_hbm, q_buf, qc_sem.at[0]),
        pltpu.make_async_copy(ct_hbm, ct_buf, qc_sem.at[1]),
    ]
    for copy in loads:
        copy.start()
    for copy in small:
        copy.wait()
    low = x_ref[:, :half].astype(F32)
    high = x_ref[:, half:].astype(F32)
    first = c == 0
    own = jnp.where(first, low, high)
    xs[...] = jnp.where(first, high, low)
    pl.semaphore_wait(barrier, 9 + jnp.where(edge, 2, 0))

    pending = []

    def send(copy, when=None):
        pending.append((when, copy))
        if when is None:
            copy.start()
        else:
            pl.when(when)(copy.start)

    send(remote(xs, xr, x_ss, x_rs, partner))
    x_copy = pending[-1][1]
    x_copy.wait_recv()
    got = xr[...]
    mine = pl.ds(pl.multiple_of((a * 4 + y) * ROWS, ROWS), ROWS)
    g[mine, :] = jnp.concatenate(
        [jnp.where(first, own, got), jnp.where(first, got, own)], axis=0
    ).astype(BF16)

    def shard(a_, y_, h):
        y_ = lax.rem(y_ + 8, 4)
        at = pl.ds(pl.multiple_of((a_ * 4 + y_) * ROWS, ROWS), ROWS)
        return g.at[at, h * quarter : (h + 1) * quarter]

    def y_send(k, h):
        piece = shard(a_of[k], y, h)
        send(remote(piece, piece, ys_ss.at[k, h, 0], y_rs.at[k, h, 0], dev(y_=y + 1)))
        send(remote(piece, piece, ys_ss.at[k, h, 1], y_rs.at[k, h, 1], dev(y_=y - 1)))

    def y_wait(k, h, side):
        piece = shard(a_of[k], y - 1 if side == 0 else y + 1, h)
        remote(piece, piece, ys_ss.at[k, h, side], y_rs.at[k, h, side], partner).wait_recv()

    def y_forward(k):
        for side in range(2):
            y_wait(k, side, side)
            piece = shard(a_of[k], y - 1 if side == 0 else y + 1, side)
            to = dev(y_=y + 1 if side == 0 else y - 1)
            send(remote(piece, piece, yf_ss.at[k, side], yf_rs.at[k, side], to))

    def y_finish(k):
        for side in range(2):
            y_wait(k, 1 - side, side)
        for side in range(2):
            piece = shard(a_of[k], y + 2, side)
            remote(piece, piece, yf_ss.at[k, side], yf_rs.at[k, side], partner).wait_recv()

    def z_wait(k, h):
        piece = shard(a_of[k], y, h)
        remote(piece, piece, zf_ss.at[0, h], z_rs.at[k, h], partner).wait_recv()

    last = l == 3
    far = jnp.where(last, 0, 3)
    side_a = jnp.where(last, a + 1, a - 1)
    beyond = dev(a_=side_a, l_=far)
    targets = [(beyond, 1), (dev(a_=side_a, l_=jnp.where(last, 2, 1)), 1)]
    for h in range(2):
        piece = shard(a, y, h)
        to, k = targets[0]
        send(remote(piece, piece, zo_ss.at[0, h], z_rs.at[k, h], to), edge)
        y_send(0, h)
    for h in range(2):
        piece = shard(a, y, h)
        to, k = targets[1]
        send(remote(piece, piece, zo_ss.at[1, h], z_rs.at[k, h], to), edge)
    send(remote(kw_ref.at[their_rows, :], wb.at[:, 2 * HEAD : 3 * HEAD], w_ss.at[0], w_rs.at[0], partner))
    send(remote(vw_ref.at[their_rows, :], wb.at[:, 3 * HEAD : 4 * HEAD], w_ss.at[1], w_rs.at[1], partner))
    w_copies = [pending[-2][1], pending[-1][1]]

    loads[2].wait()
    q_gain = qg_ref[pl.ds(layer, 1), :]
    k_gain = kg_ref[pl.ds(layer, 1), :]

    def norm_queries(h, carry):
        at = pl.ds(pl.multiple_of(h * HEAD, HEAD), HEAD)
        raw_q = q_buf[:, at].astype(F32)
        scale = lax.rsqrt(jnp.mean(raw_q * raw_q, axis=-1, keepdims=True) + EPSILON)
        normed = raw_q * scale
        qn_buf[:, at] = normed
        qs_buf[:, at] = (normed * q_gain).astype(BF16)
        return carry

    lax.fori_loop(0, heads, norm_queries, 0)
    row_doc = jnp.broadcast_to(rd_ref[...].astype(F32), (rows, rows)).T
    mask[...] = jnp.where(row_doc == td_ref[...].astype(F32), 1.0, 0.0)

    y_forward(0)
    for h in range(2):
        z_wait(1, h)
        piece = shard(a_of[1], y, h)
        send(remote(piece, piece, zf_ss.at[0, h], z_rs.at[2, h], dev(l_=mate)))
        y_send(1, h)

    def project(k):
        y_finish(k)
        at = pl.ds(pl.multiple_of(a_of[k] * block, block), block)
        out = jnp.dot(g[at, :], wb[...], preferred_element_type=F32)
        raw[at, :] = out[:, : 2 * HEAD]
        raw_send[at, :] = out[:, 2 * HEAD :]
        send(remote(raw_send.at[at, :], raw_recv.at[at, :], pr_ss.at[k], pr_rs.at[k], partner))

    loads[0].wait()
    loads[1].wait()
    for copy in w_copies:
        copy.wait_recv()
    loads[3].wait()
    project(0)
    for h in range(2):
        z_wait(2, h)
        piece = shard(a_of[2], y, h)
        send(remote(piece, piece, zo_ss.at[2, h], z_rs.at[3, h], beyond), edge)
        y_send(2, h)
    y_forward(1)
    for h in range(2):
        z_wait(3, h)
        piece = shard(a_of[3], y, h)
        send(remote(piece, piece, zf_ss.at[1, h], z_rs.at[3, h], dev(l_=mate)), edge)
        y_send(3, h)
    y_forward(2)
    project(1)
    y_forward(3)
    project(2)
    project(3)

    for k in range(4):
        at = pl.ds(pl.multiple_of(a_of[k] * block, block), block)
        remote(raw_send.at[at, :], raw_recv.at[at, :], pr_ss.at[k], pr_rs.at[k], partner).wait_recv()
    projected = raw[...] + raw_recv[...]
    key_raw = projected[:, :HEAD]
    values = projected[:, HEAD:].astype(BF16)
    key_scale = lax.rsqrt(jnp.mean(key_raw * key_raw, axis=-1, keepdims=True) + EPSILON)
    key_normed = key_raw * key_scale
    keys = (key_normed * k_gain).astype(BF16)
    factor = 1.0 / math.sqrt(HEAD)
    nt = (((1,), (1,)), ((), ()))
    tn = (((0,), (0,)), ((), ()))

    def head(h, carry):
        grad_key, grad_value, gain = carry
        at = pl.ds(pl.multiple_of(h * HEAD, HEAD), HEAD)
        query = qs_buf[:, at]
        upstream = ct_buf[:, at]
        scores = lax.dot_general(keys, query, nt, preferred_element_type=F32) * factor
        exponents = jnp.exp(scores) * mask[...]
        softmax = exponents * (1.0 / jnp.sum(exponents, axis=0, keepdims=True))
        grad_softmax = lax.dot_general(values, upstream, nt, preferred_element_type=F32)
        inner = jnp.sum(softmax * grad_softmax, axis=0, keepdims=True)
        grad_scores = (softmax * (grad_softmax - inner)).astype(BF16)
        grad_value = grad_value + jnp.dot(softmax.astype(BF16), upstream, preferred_element_type=F32)
        grad_key = grad_key + jnp.dot(grad_scores, query, preferred_element_type=F32)
        grad_query = lax.dot_general(grad_scores, keys, tn, preferred_element_type=F32)
        gain = gain + jnp.sum(grad_query * qn_buf[:, at], axis=0, keepdims=True)
        return grad_key, grad_value, gain

    zero = jnp.zeros((rows, HEAD), F32)
    grad_key, grad_value, gain_query = lax.fori_loop(
        0, heads, head, (zero, zero, jnp.zeros((1, HEAD), F32))
    )
    grad_key = grad_key * factor
    scaled_up = grad_key * k_gain
    key_back = key_scale * (
        scaled_up - key_normed * jnp.mean(scaled_up * key_normed, axis=-1, keepdims=True)
    )
    kv[:, :HEAD] = key_back.astype(BF16)
    kv[:, HEAD : 2 * HEAD] = grad_value.astype(BF16)
    kv_copy = remote(kv.at[:, : 2 * HEAD], kv.at[:, 2 * HEAD :], kv_ss, kv_rs, partner)
    send(kv_copy)

    gain_a[l] = jnp.concatenate(
        [
            jnp.sum(grad_key * key_normed, axis=0, keepdims=True),
            gain_query * factor,
            jnp.zeros((6, HEAD), F32),
        ],
        axis=0,
    )
    for d in range(1, 4):
        to = dev(l_=lax.rem(l + d, 4))
        send(remote(gain_a.at[l], gain_a.at[l], ga_ss.at[d - 1], ga_rs.at[d - 1], to))
    kv_copy.wait_recv()

    b_of = [lax.rem(a + 2, 4), lax.rem(a + 1, 4), lax.rem(a + 3, 4), a]
    y_up, y_down = dev(y_=y + 1), dev(y_=y - 1)

    def part(b, y_, h):
        y_ = lax.rem(y_ + 8, 4)
        at = pl.ds(pl.multiple_of((b * 4 + y_) * ROWS, ROWS), ROWS)
        return p.at[at, h * quarter : (h + 1) * quarter]

    def terms(k):
        b = b_of[k]
        at = pl.ds(pl.multiple_of(b * block, block), block)
        left = kv[at, :]
        for h in range(2):
            cols = slice(h * quarter, (h + 1) * quarter)
            p[at, cols] = lax.dot_general(
                left, wb[cols, :], nt, preferred_element_type=F32
            ).astype(BF16)

    def opposite(k):
        b = b_of[k]
        for h in range(2):
            send(remote(part(b, y + 2, h), y1.at[h, k], r1_ss.at[h, k], r1_rs.at[h, k], y_up if h == 0 else y_down))

    def beside(k):
        b = b_of[k]
        for h in range(2):
            src = part(b, y + 1, 1) if h == 0 else part(b, y - 1, 0)
            dst = y2.at[h, k, 1 - h]
            send(remote(src, dst, r2_ss.at[h, k], r2_rs.at[h, k], y_up if h == 0 else y_down))

    def pass_on(k):
        b = b_of[k]
        for h in range(2):
            remote(y1.at[h, k], y1.at[h, k], r1_ss.at[h, k], r1_rs.at[h, k], partner).wait_recv()
            mine_ = part(b, y + 1, 0) if h == 0 else part(b, y - 1, 1)
            ysum[h, k] = (mine_[...].astype(F32) + y1[h, k].astype(F32)).astype(BF16)
            send(remote(ysum.at[h, k], y2.at[h, k, h], r3_ss.at[h, k], r3_rs.at[h, k], y_up if h == 0 else y_down))

    active = c == l // 2

    def group(k):
        b = b_of[k]
        for h in range(2):
            remote(y2.at[h, k, 1 - h], y2.at[h, k, 1 - h], r2_ss.at[h, k], r2_rs.at[h, k], partner).wait_recv()
            remote(y2.at[h, k, h], y2.at[h, k, h], r3_ss.at[h, k], r3_rs.at[h, k], partner).wait_recv()
        for i in range(2):
            yred[k, i] = (
                part(b, y, i)[...].astype(F32) + y2[0, k, i].astype(F32) + y2[1, k, i].astype(F32)
            ).astype(BF16)
            to = 2 * c + i
            slot = lax.rem(l - to + 4, 4)
            slot_ = jnp.maximum(slot - 1, 0)
            send(
                remote(yred.at[k, i], zin.at[k, slot_], in_ss.at[k, i], in_rs.at[k, slot_], dev(l_=to)),
                to != l,
            )

    def group_sum(k):
        for d in range(3):
            remote(zin.at[k, d], zin.at[k, d], in_ss.at[k, 0], in_rs.at[k, d], partner).wait_recv()
        total = jnp.where(even, yred[k, 0].astype(F32), yred[k, 1].astype(F32))
        for d in range(3):
            total = total + zin[k, d].astype(F32)
        return total

    def across(k):
        @pl.when(active)
        def _():
            zred[k] = group_sum(k).astype(BF16)
            z4_copy(k).start()

    def z4_copy(k):
        return remote(zred.at[k], zf.at[k], z4_ss.at[k], z4_rs.at[k], dev(a_=b_of[k]))

    terms(0)
    opposite(0)
    beside(0)
    terms(1)
    opposite(1)
    pass_on(0)
    beside(1)
    terms(2)
    opposite(2)
    pass_on(1)
    beside(2)
    terms(3)
    opposite(3)

    for d in range(1, 4):
        src = gain_a.at[lax.rem(l - d + 4, 4)]
        remote(src, src, ga_ss.at[d - 1], ga_rs.at[d - 1], partner).wait_recv()
    gain_b[xi] = gain_a[0] + gain_a[1] + gain_a[2] + gain_a[3]
    for d in range(1, 4):
        to = dev(x_=lax.rem(xi + d, 4))
        send(remote(gain_b.at[xi], gain_b.at[xi], gb_ss.at[d - 1], gb_rs.at[d - 1], to))

    group(0)
    pass_on(2)
    beside(3)
    group(1)
    across(0)
    pass_on(3)
    group(2)
    across(1)
    group(3)
    across(2)

    for d in range(1, 4):
        src = gain_b.at[lax.rem(xi - d + 4, 4)]
        remote(src, src, gb_ss.at[d - 1], gb_rs.at[d - 1], partner).wait_recv()
    gains = gain_b[0] + gain_b[1] + gain_b[2] + gain_b[3]
    gk_out[...] = gains[0:1]
    gq_out[...] = gains[1:2]

    f_copy = remote(fs, fr, f_ss, f_rs, partner)

    @pl.when(active)
    def _():
        total = group_sum(3)
        for k in range(3):
            z4_copy(k).wait_recv()
            total = total + zf[k].astype(F32)
        top, bottom = total[: ROWS // 2], total[ROWS // 2 :]
        fs[...] = jnp.where(first, bottom, top)
        f_copy.start()
        out_ref[...] = jnp.where(first, top, bottom).astype(BF16)
        for k in range(3):
            z4_copy(k).wait_send()
        f_copy.wait_send()

    @pl.when(jnp.logical_not(active))
    def _():
        f_copy.wait_recv()
        out_ref[...] = fr[...].astype(BF16)

    for when, copy in pending:
        if when is None:
            copy.wait_send()
        else:
            pl.when(when)(copy.wait_send)


def on_device(
    image_rows,
    key_weight,
    value_weight,
    key_gain,
    query_gain,
    queries,
    cotangent,
    text_doc,
    row_doc,
):
    width = image_rows.shape[2]
    half = width // 2
    quarter = half // 2
    tok = queries.shape[2]
    q_width = queries.shape[3]
    rows = row_doc.shape[1]
    vmem = pl.BlockSpec(memory_space=pltpu.VMEM)
    hbm = pl.BlockSpec(memory_space=pltpu.HBM)
    dma = pltpu.SemaphoreType.DMA
    scratch = [
        pltpu.VMEM((8, width), BF16),
        pltpu.VMEM(key_gain.shape, F32),
        pltpu.VMEM(query_gain.shape, F32),
        pltpu.VMEM(text_doc.shape, jnp.int32),
        pltpu.VMEM(row_doc.shape, jnp.int32),
        pltpu.VMEM((half, 4 * HEAD), BF16),
        pltpu.VMEM((tok, q_width), BF16),
        pltpu.VMEM((tok, q_width), BF16),
        pltpu.VMEM((tok, q_width), BF16),
        pltpu.VMEM((tok, q_width), F32),
        pltpu.VMEM((8, half), F32),
        pltpu.VMEM((8, half), F32),
        pltpu.VMEM((rows, half), BF16),
        pltpu.VMEM((rows, 2 * HEAD), F32),
        pltpu.VMEM((rows, 2 * HEAD), F32),
        pltpu.VMEM((rows, 2 * HEAD), F32),
        pltpu.VMEM((rows, 4 * HEAD), BF16),
        pltpu.VMEM((rows, half), BF16),
        pltpu.VMEM((2, 4, ROWS, quarter), BF16),
        pltpu.VMEM((2, 4, 2, ROWS, quarter), BF16),
        pltpu.VMEM((2, 4, ROWS, quarter), BF16),
        pltpu.VMEM((4, 2, ROWS, quarter), BF16),
        pltpu.VMEM((4, 3, ROWS, quarter), BF16),
        pltpu.VMEM((3, ROWS, quarter), BF16),
        pltpu.VMEM((3, ROWS, quarter), BF16),
        pltpu.VMEM((8, quarter), F32),
        pltpu.VMEM((8, quarter), F32),
        pltpu.VMEM((4, 8, HEAD), F32),
        pltpu.VMEM((4, 8, HEAD), F32),
        pltpu.VMEM((rows, tok), F32),
        dma((5,)), dma((2,)), dma((2,)), dma((2,)), dma((2,)), dma, dma,
        dma((3, 2)), dma((2, 2)), dma((4, 2)),
        dma((4, 2, 2)), dma((4, 2, 2)), dma((4, 2)), dma((4, 2)),
        dma((4,)), dma((4,)), dma, dma,
        dma((2, 4)), dma((2, 4)), dma((2, 4)), dma((2, 4)), dma((2, 4)), dma((2, 4)),
        dma((4, 2)), dma((4, 3)), dma((3,)), dma((3,)), dma, dma,
        dma((3,)), dma((3,)), dma((3,)), dma((3,)),
    ]
    grad, gain_key, gain_query = pl.pallas_call(
        kernel,
        name="image_row_gradients",
        out_shape=(
            jax.ShapeDtypeStruct((8, quarter), BF16),
            jax.ShapeDtypeStruct((1, HEAD), F32),
            jax.ShapeDtypeStruct((1, HEAD), F32),
        ),
        in_specs=[hbm] * 9,
        out_specs=(vmem, vmem, vmem),
        scratch_shapes=scratch,
        compiler_params=pltpu.CompilerParams(
            collective_id=0, has_side_effects=True, vmem_limit_bytes=62 * 1024 * 1024
        ),
    )(
        image_rows[0], key_weight[0], value_weight[0], key_gain, query_gain,
        queries[0, 0], cotangent[0, 0], text_doc, row_doc,
    )
    return (grad[None], gain_key, gain_query)


def solution(mesh):
    in_specs = (
        P("dp", "section", None),
        P("section", None, "tensor"),
        P("section", None, "tensor"),
        P(),
        P(),
        P("dp", "section", None, "tensor"),
        P("dp", "section", None, "tensor"),
        P("dp", None),
        P("dp", None),
    )
    out_specs = (P("dp", "section", "tensor"), P("section", None), P("section", None))
    return jax.shard_map(
        on_device, mesh=mesh, in_specs=in_specs, out_specs=out_specs, check_vma=False
    )
```

```python
import math

import jax
import jax.numpy as jnp
from jax import lax
from jax.experimental import pallas as pl
from jax.experimental.pallas import tpu as pltpu
from jax.sharding import PartitionSpec as P

HEAD = 128
EPSILON = 1e-05
MESH = pl.DeviceIdType.MESH
F32 = jnp.float32
BF16 = jnp.bfloat16
ROWS = 16


def kernel(
    x_hbm, kw_ref, vw_ref, kg_hbm, qg_hbm, q_hbm, ct_hbm, td_hbm, rd_hbm,
    out_ref, gk_out, gq_out,
    x_ref, kg_ref, qg_ref, td_ref, rd_ref,
    wb, wm, q_buf, ct_buf, qs_buf, qn_buf, xs, xr, g, raw, raw_send, raw_recv, kv, p,
    y1, y2, ysum, yred, zin, fs, fr, gain_a, gain_b, mask,
    s_sem, w_sem, w_ss, w_rs, wz_ss, wz_rs, wx_ss, wx_rs, wf_ss, wf_rs, qc_sem, x_ss, x_rs, zo_ss, zf_ss, z_rs, ys_ss, y_rs, yf_ss, yf_rs,
    pr_ss, pr_rs, kv_ss, kv_rs, r1_ss, r1_rs, r2_ss, r2_rs, r3_ss, r3_rs,
    in_ss, in_rs, f_ss, f_rs, ga_ss, ga_rs, gb_ss, gb_rs,
):
    s = lax.axis_index("section")
    l = lax.axis_index("tensor")
    xi = lax.axis_index("dp")
    a = s // 8
    y = (s // 2) % 4
    c = s % 2
    half = g.shape[1]
    quarter = half // 2
    tok = q_buf.shape[0]
    heads = q_buf.shape[1] // HEAD
    rows = g.shape[0]
    block = 4 * ROWS
    layer = s // 2

    def dev(a_=None, y_=None, c_=None, l_=None, x_=None):
        a_ = a if a_ is None else lax.rem(a_ + 8, 4)
        y_ = y if y_ is None else lax.rem(y_ + 8, 4)
        c_ = c if c_ is None else c_
        return {
            "section": (a_ * 4 + y_) * 2 + c_,
            "tensor": l if l_ is None else l_,
            "dp": xi if x_ is None else x_,
        }

    def remote(src, dst, ss, rs, to):
        return pltpu.make_async_remote_copy(
            src_ref=src, dst_ref=dst, send_sem=ss, recv_sem=rs, device_id=to, device_id_type=MESH
        )

    partner = dev(c_=1 - c)
    edge = jnp.logical_or(l == 0, l == 3)
    even = lax.rem(l, 2) == 0
    mate = jnp.where(even, l + 1, l - 1)
    step = jnp.where(even, 1, -1)
    a_of = [a, lax.rem(a - step + 4, 4), lax.rem(a + step + 4, 4), lax.rem(a + 2, 4)]

    small = [
        pltpu.make_async_copy(src, dst, s_sem.at[i])
        for i, (src, dst) in enumerate(
            [(x_hbm, x_ref), (kg_hbm, kg_ref), (qg_hbm, qg_ref), (td_hbm, td_ref), (rd_hbm, rd_ref)]
        )
    ]
    for copy in small:
        copy.start()

    barrier = pltpu.get_barrier_semaphore()

    def greet(to):
        pl.semaphore_signal(barrier, inc=1, device_id=to, device_id_type=MESH)

    greet(partner)
    greet(dev(y_=y + 1))
    greet(dev(y_=y - 1))
    for d in range(1, 4):
        greet(dev(l_=lax.rem(l + d, 4)))
        greet(dev(x_=lax.rem(xi + d, 4)))

    greet(dev(l_=mate, c_=1 - c))
    greet(dev(a_=a - step, l_=jnp.where(even, 3, 0)))

    own_rows = pl.ds(pl.multiple_of(c * half, 128), half)
    their_rows = pl.ds(pl.multiple_of((1 - c) * half, 128), half)
    loads = [
        pltpu.make_async_copy(kw_ref.at[own_rows, :], wb.at[:, 0:HEAD], w_sem.at[0]),
        pltpu.make_async_copy(vw_ref.at[own_rows, :], wb.at[:, HEAD : 2 * HEAD], w_sem.at[1]),
        pltpu.make_async_copy(q_hbm, q_buf, qc_sem.at[0]),
        pltpu.make_async_copy(ct_hbm, ct_buf, qc_sem.at[1]),
    ]
    for copy in loads:
        copy.start()
    for copy in small:
        copy.wait()
    low = x_ref[:, :half].astype(F32)
    high = x_ref[:, half:].astype(F32)
    first = c == 0
    own = jnp.where(first, low, high)
    xs[...] = jnp.where(first, high, low)
    pl.semaphore_wait(barrier, 10 + jnp.where(edge, 2, 0))

    pending = []

    def send(copy, when=None):
        pending.append((when, copy))
        if when is None:
            copy.start()
        else:
            pl.when(when)(copy.start)

    share = quarter // 4

    def to_mate(i):
        core = c if i == 0 else 1 - c
        start = (2 * core + lax.rem(mate, 2)) * quarter + xi * share
        src_rows = pl.ds(pl.multiple_of(start, ROWS), share)
        dst_rows = pl.ds(pl.multiple_of(xi * share, ROWS), share)
        for j, ref in enumerate((kw_ref, vw_ref)):
            n = 2 * i + j
            dst = wm.at[dst_rows, n * HEAD : (n + 1) * HEAD]
            send(remote(ref.at[src_rows, :], dst, wz_ss.at[n], wz_rs.at[n], dev(l_=mate, c_=core)))

    def piece_of(x_, i):
        at = pl.ds(pl.multiple_of(lax.rem(x_ + 4, 4) * share, ROWS), share)
        return wm.at[at, 2 * i * HEAD : 2 * (i + 1) * HEAD]

    x_up, x_down = dev(x_=lax.rem(xi + 1, 4)), dev(x_=lax.rem(xi + 3, 4))

    def to_dp(i):
        for n in (2 * i, 2 * i + 1):
            at = pl.ds(pl.multiple_of(xi * share, ROWS), share)
            dst = wm.at[at, n * HEAD : (n + 1) * HEAD]
            remote(dst, dst, wz_ss.at[n], wz_rs.at[n], partner).wait_recv()
        own_piece = piece_of(xi, i)
        send(remote(own_piece, own_piece, wx_ss.at[i, 0], wx_rs.at[i, 0], x_up))
        send(remote(own_piece, own_piece, wx_ss.at[i, 1], wx_rs.at[i, 1], x_down))

    def dp_wait(i, side):
        part_ = piece_of(xi - 1 if side == 0 else xi + 1, i)
        remote(part_, part_, wx_ss.at[i, side], wx_rs.at[i, side], partner).wait_recv()

    def dp_forward(i):
        dp_wait(i, i)
        part_ = piece_of(xi - 1 if i == 0 else xi + 1, i)
        send(remote(part_, part_, wf_ss.at[i], wf_rs.at[i], x_up if i == 0 else x_down))

    def dp_finish():
        for i in range(2):
            dp_wait(i, 1 - i)
            part_ = piece_of(xi + 2, i)
            remote(part_, part_, wf_ss.at[i], wf_rs.at[i], partner).wait_recv()

    to_mate(0)
    send(remote(xs, xr, x_ss, x_rs, partner))
    x_copy = pending[-1][1]
    x_copy.wait_recv()
    got = xr[...]
    mine = pl.ds(pl.multiple_of((a * 4 + y) * ROWS, ROWS), ROWS)
    g[mine, :] = jnp.concatenate(
        [jnp.where(first, own, got), jnp.where(first, got, own)], axis=0
    ).astype(BF16)

    def shard(a_, y_, h):
        y_ = lax.rem(y_ + 8, 4)
        at = pl.ds(pl.multiple_of((a_ * 4 + y_) * ROWS, ROWS), ROWS)
        return g.at[at, h * quarter : (h + 1) * quarter]

    def y_send(k, h):
        piece = shard(a_of[k], y, h)
        send(remote(piece, piece, ys_ss.at[k, h, 0], y_rs.at[k, h, 0], dev(y_=y + 1)))
        send(remote(piece, piece, ys_ss.at[k, h, 1], y_rs.at[k, h, 1], dev(y_=y - 1)))

    def y_wait(k, h, side):
        piece = shard(a_of[k], y - 1 if side == 0 else y + 1, h)
        remote(piece, piece, ys_ss.at[k, h, side], y_rs.at[k, h, side], partner).wait_recv()

    def y_forward(k):
        for side in range(2):
            y_wait(k, side, side)
            piece = shard(a_of[k], y - 1 if side == 0 else y + 1, side)
            to = dev(y_=y + 1 if side == 0 else y - 1)
            send(remote(piece, piece, yf_ss.at[k, side], yf_rs.at[k, side], to))

    def y_finish(k):
        for side in range(2):
            y_wait(k, 1 - side, side)
        for side in range(2):
            piece = shard(a_of[k], y + 2, side)
            remote(piece, piece, yf_ss.at[k, side], yf_rs.at[k, side], partner).wait_recv()

    def z_wait(k, h):
        piece = shard(a_of[k], y, h)
        remote(piece, piece, zf_ss.at[0, h], z_rs.at[k, h], partner).wait_recv()

    last = l == 3
    far = jnp.where(last, 0, 3)
    side_a = jnp.where(last, a + 1, a - 1)
    beyond = dev(a_=side_a, l_=far)
    targets = [(beyond, 1), (dev(a_=side_a, l_=jnp.where(last, 2, 1)), 1)]
    for h in range(2):
        piece = shard(a, y, h)
        to, k = targets[0]
        send(remote(piece, piece, zo_ss.at[0, h], z_rs.at[k, h], to), edge)
        y_send(0, h)
    for h in range(2):
        piece = shard(a, y, h)
        to, k = targets[1]
        send(remote(piece, piece, zo_ss.at[1, h], z_rs.at[k, h], to), edge)
    send(remote(kw_ref.at[their_rows, :], wb.at[:, 2 * HEAD : 3 * HEAD], w_ss.at[0], w_rs.at[0], partner))
    send(remote(vw_ref.at[their_rows, :], wb.at[:, 3 * HEAD : 4 * HEAD], w_ss.at[1], w_rs.at[1], partner))
    w_copies = [pending[-2][1], pending[-1][1]]
    to_mate(1)

    loads[2].wait()
    q_gain = qg_ref[pl.ds(layer, 1), :]
    k_gain = kg_ref[pl.ds(layer, 1), :]

    def norm_queries(h, carry):
        at = pl.ds(pl.multiple_of(h * HEAD, HEAD), HEAD)
        raw_q = q_buf[:, at].astype(F32)
        scale = lax.rsqrt(jnp.mean(raw_q * raw_q, axis=-1, keepdims=True) + EPSILON)
        normed = raw_q * scale
        qn_buf[:, at] = normed
        qs_buf[:, at] = (normed * q_gain).astype(BF16)
        return carry

    lax.fori_loop(0, heads, norm_queries, 0)
    row_doc = jnp.broadcast_to(rd_ref[...].astype(F32), (rows, rows)).T
    mask[...] = jnp.where(row_doc == td_ref[...].astype(F32), 1.0, 0.0)

    y_forward(0)
    for h in range(2):
        z_wait(1, h)
        piece = shard(a_of[1], y, h)
        send(remote(piece, piece, zf_ss.at[0, h], z_rs.at[2, h], dev(l_=mate)))
        y_send(1, h)

    def project(k):
        y_finish(k)
        at = pl.ds(pl.multiple_of(a_of[k] * block, block), block)
        out = jnp.dot(g[at, :], wb[...], preferred_element_type=F32)
        raw[at, :] = out[:, : 2 * HEAD]
        raw_send[at, :] = out[:, 2 * HEAD :]
        send(remote(raw_send.at[at, :], raw_recv.at[at, :], pr_ss.at[k], pr_rs.at[k], partner))

    to_dp(0)
    loads[0].wait()
    loads[1].wait()
    for copy in w_copies:
        copy.wait_recv()
    loads[3].wait()
    project(0)
    for h in range(2):
        z_wait(2, h)
        piece = shard(a_of[2], y, h)
        send(remote(piece, piece, zo_ss.at[2, h], z_rs.at[3, h], beyond), edge)
        y_send(2, h)
    y_forward(1)
    to_dp(1)
    for h in range(2):
        z_wait(3, h)
        piece = shard(a_of[3], y, h)
        send(remote(piece, piece, zf_ss.at[1, h], z_rs.at[3, h], dev(l_=mate)), edge)
        y_send(3, h)
    y_forward(2)
    dp_forward(0)
    project(1)
    y_forward(3)
    dp_forward(1)
    project(2)
    project(3)

    for k in range(4):
        at = pl.ds(pl.multiple_of(a_of[k] * block, block), block)
        remote(raw_send.at[at, :], raw_recv.at[at, :], pr_ss.at[k], pr_rs.at[k], partner).wait_recv()
    projected = raw[...] + raw_recv[...]
    key_raw = projected[:, :HEAD]
    values = projected[:, HEAD:].astype(BF16)
    key_scale = lax.rsqrt(jnp.mean(key_raw * key_raw, axis=-1, keepdims=True) + EPSILON)
    key_normed = key_raw * key_scale
    keys = (key_normed * k_gain).astype(BF16)
    factor = 1.0 / math.sqrt(HEAD)
    nt = (((1,), (1,)), ((), ()))
    tn = (((0,), (0,)), ((), ()))

    def head(h, carry):
        grad_key, grad_value, gain = carry
        at = pl.ds(pl.multiple_of(h * HEAD, HEAD), HEAD)
        query = qs_buf[:, at]
        upstream = ct_buf[:, at]
        scores = lax.dot_general(keys, query, nt, preferred_element_type=F32) * factor
        exponents = jnp.exp(scores) * mask[...]
        softmax = exponents * (1.0 / jnp.sum(exponents, axis=0, keepdims=True))
        grad_softmax = lax.dot_general(values, upstream, nt, preferred_element_type=F32)
        inner = jnp.sum(softmax * grad_softmax, axis=0, keepdims=True)
        grad_scores = (softmax * (grad_softmax - inner)).astype(BF16)
        grad_value = grad_value + jnp.dot(softmax.astype(BF16), upstream, preferred_element_type=F32)
        grad_key = grad_key + jnp.dot(grad_scores, query, preferred_element_type=F32)
        grad_query = lax.dot_general(grad_scores, keys, tn, preferred_element_type=F32)
        gain = gain + jnp.sum(grad_query * qn_buf[:, at], axis=0, keepdims=True)
        return grad_key, grad_value, gain

    zero = jnp.zeros((rows, HEAD), F32)
    grad_key, grad_value, gain_query = lax.fori_loop(
        0, heads, head, (zero, zero, jnp.zeros((1, HEAD), F32)), unroll=4
    )
    grad_key = grad_key * factor
    scaled_up = grad_key * k_gain
    key_back = key_scale * (
        scaled_up - key_normed * jnp.mean(scaled_up * key_normed, axis=-1, keepdims=True)
    )
    kv[:, :HEAD] = key_back.astype(BF16)
    kv[:, HEAD : 2 * HEAD] = grad_value.astype(BF16)
    b_of = [lax.rem(a + 2, 4), lax.rem(a + 1, 4), lax.rem(a + 3, 4), a]
    kv_to = [partner, dev(l_=mate), dev(l_=mate, c_=1 - c)]

    def kv_copy(k, i):
        at = pl.ds(pl.multiple_of(b_of[k] * block, block), block)
        dst = kv.at[at, 2 * (i + 1) * HEAD : 2 * (i + 2) * HEAD]
        return remote(kv.at[at, : 2 * HEAD], dst, kv_ss.at[k, i], kv_rs.at[k, i], kv_to[i])

    for k in range(4):
        for i in range(3):
            send(kv_copy(k, i))

    gain_a[l] = jnp.concatenate(
        [
            jnp.sum(grad_key * key_normed, axis=0, keepdims=True),
            gain_query * factor,
            jnp.zeros((6, HEAD), F32),
        ],
        axis=0,
    )
    for d in range(1, 4):
        to = dev(l_=lax.rem(l + d, 4))
        send(remote(gain_a.at[l], gain_a.at[l], ga_ss.at[d - 1], ga_rs.at[d - 1], to))

    y_up, y_down = dev(y_=y + 1), dev(y_=y - 1)
    split = quarter // 2 // HEAD * HEAD + HEAD
    cols = [slice(0, split), slice(split, quarter)]
    width = [split, quarter - split]
    w_rows = pl.ds(pl.multiple_of(lax.rem(l, 2) * quarter, ROWS), quarter)

    def part(b, y_, h=None):
        y_ = lax.rem(y_ + 8, 4)
        at = pl.ds(pl.multiple_of((b * 4 + y_) * ROWS, ROWS), ROWS)
        return p.at[at, :] if h is None else p.at[at, cols[h]]

    def y1_at(h, k):
        return y1.at[h, k, :, : width[h]]

    def terms(k):
        for i in range(3):
            kv_copy(k, i).wait_recv()
        at = pl.ds(pl.multiple_of(b_of[k] * block, block), block)
        p[at, :] = (
            lax.dot_general(kv[at, : 4 * HEAD], wb[w_rows, :], nt, preferred_element_type=F32)
            + lax.dot_general(kv[at, 4 * HEAD :], wm[...], nt, preferred_element_type=F32)
        ).astype(BF16)

    def opposite(k):
        b = b_of[k]
        for h in range(2):
            send(remote(part(b, y + 2, h), y1_at(h, k), r1_ss.at[h, k], r1_rs.at[h, k], y_up if h == 0 else y_down))

    def beside(k):
        b = b_of[k]
        for h in range(2):
            src = part(b, y + 1, 1) if h == 0 else part(b, y - 1, 0)
            dst = y2.at[h, k, :, cols[1 - h]]
            send(remote(src, dst, r2_ss.at[h, k], r2_rs.at[h, k], y_up if h == 0 else y_down))

    def pass_on(k):
        b = b_of[k]
        for h in range(2):
            remote(y1_at(h, k), y1_at(h, k), r1_ss.at[h, k], r1_rs.at[h, k], partner).wait_recv()
            mine_ = part(b, y + 1, 0) if h == 0 else part(b, y - 1, 1)
            total = ysum.at[h, k, :, : width[h]]
            total[...] = (mine_[...].astype(F32) + y1_at(h, k)[...].astype(F32)).astype(BF16)
            send(remote(total, y2.at[h, k, :, cols[h]], r3_ss.at[h, k], r3_rs.at[h, k], y_up if h == 0 else y_down))

    active = c == l // 2

    owner = jnp.where(active, l, lax.rem(l + 2, 4))
    slot = jnp.where(active, 0, 1)

    def group(k):
        b = b_of[k]
        for h in range(2):
            for sem_s, sem_r, i in ((r2_ss, r2_rs, 1 - h), (r3_ss, r3_rs, h)):
                dst = y2.at[h, k, :, cols[i]]
                remote(dst, dst, sem_s.at[h, k], sem_r.at[h, k], partner).wait_recv()
        total = part(b, y)[...].astype(F32) + y2[0, k].astype(F32) + y2[1, k].astype(F32)
        yred[k] = total.astype(BF16)
        to = dev(a_=b, l_=owner)
        copy = remote(yred.at[k], zin.at[k, slot], in_ss.at[k], in_rs.at[k, slot], to)
        send(copy, jnp.logical_not(active) if k == 3 else None)

    dp_finish()
    terms(0)
    opposite(0)
    beside(0)
    terms(1)
    opposite(1)
    pass_on(0)
    beside(1)
    terms(2)
    opposite(2)
    pass_on(1)
    beside(2)
    terms(3)
    opposite(3)

    for d in range(1, 4):
        src = gain_a.at[lax.rem(l - d + 4, 4)]
        remote(src, src, ga_ss.at[d - 1], ga_rs.at[d - 1], partner).wait_recv()
    gain_b[xi] = gain_a[0] + gain_a[1] + gain_a[2] + gain_a[3]
    for d in range(1, 4):
        to = dev(x_=lax.rem(xi + d, 4))
        send(remote(gain_b.at[xi], gain_b.at[xi], gb_ss.at[d - 1], gb_rs.at[d - 1], to))

    group(0)
    pass_on(2)
    beside(3)
    group(1)
    pass_on(3)
    group(2)
    group(3)

    for d in range(1, 4):
        src = gain_b.at[lax.rem(xi - d + 4, 4)]
        remote(src, src, gb_ss.at[d - 1], gb_rs.at[d - 1], partner).wait_recv()
    gains = gain_b[0] + gain_b[1] + gain_b[2] + gain_b[3]
    gk_out[...] = gains[0:1]
    gq_out[...] = gains[1:2]

    f_copy = remote(fs, fr, f_ss, f_rs, partner)

    @pl.when(active)
    def _():
        total = yred[3].astype(F32)
        for k in range(4):
            for j in range(1 if k == 3 else 0, 2):
                got_ = zin.at[k, j]
                remote(got_, got_, in_ss.at[k], in_rs.at[k, j], partner).wait_recv()
                total = total + got_[...].astype(F32)
        top, bottom = total[: ROWS // 2], total[ROWS // 2 :]
        fs[...] = jnp.where(first, bottom, top)
        f_copy.start()
        out_ref[...] = jnp.where(first, top, bottom).astype(BF16)
        f_copy.wait_send()

    @pl.when(jnp.logical_not(active))
    def _():
        f_copy.wait_recv()
        out_ref[...] = fr[...].astype(BF16)

    for when, copy in pending:
        if when is None:
            copy.wait_send()
        else:
            pl.when(when)(copy.wait_send)


def hand_over(a_ref, b_ref, c_ref, a_out, b_out, c_out, sems):
    copies = [
        pltpu.make_async_copy(src, dst, sems.at[i])
        for i, (src, dst) in enumerate([(a_ref, a_out), (b_ref, b_out), (c_ref, c_out)])
    ]
    for copy in copies:
        copy.start()
    for copy in copies:
        copy.wait()


def on_device(
    image_rows,
    key_weight,
    value_weight,
    key_gain,
    query_gain,
    queries,
    cotangent,
    text_doc,
    row_doc,
):
    width = image_rows.shape[2]
    half = width // 2
    quarter = half // 2
    tok = queries.shape[2]
    q_width = queries.shape[3]
    rows = row_doc.shape[1]
    vmem = pl.BlockSpec(memory_space=pltpu.VMEM)
    hbm = pl.BlockSpec(memory_space=pltpu.HBM)
    dma = pltpu.SemaphoreType.DMA
    scratch = [
        pltpu.VMEM((8, width), BF16),
        pltpu.VMEM(key_gain.shape, F32),
        pltpu.VMEM(query_gain.shape, F32),
        pltpu.VMEM(text_doc.shape, jnp.int32),
        pltpu.VMEM(row_doc.shape, jnp.int32),
        pltpu.VMEM((half, 4 * HEAD), BF16),
        pltpu.VMEM((quarter, 4 * HEAD), BF16),
        pltpu.VMEM((tok, q_width), BF16),
        pltpu.VMEM((tok, q_width), BF16),
        pltpu.VMEM((tok, q_width), BF16),
        pltpu.VMEM((tok, q_width), F32),
        pltpu.VMEM((8, half), F32),
        pltpu.VMEM((8, half), F32),
        pltpu.VMEM((rows, half), BF16),
        pltpu.VMEM((rows, 2 * HEAD), F32),
        pltpu.VMEM((rows, 2 * HEAD), F32),
        pltpu.VMEM((rows, 2 * HEAD), F32),
        pltpu.VMEM((rows, 8 * HEAD), BF16),
        pltpu.VMEM((rows, quarter), BF16),
        pltpu.VMEM((2, 4, ROWS, quarter), BF16),
        pltpu.VMEM((2, 4, ROWS, quarter), BF16),
        pltpu.VMEM((2, 4, ROWS, quarter), BF16),
        pltpu.VMEM((4, ROWS, quarter), BF16),
        pltpu.VMEM((4, 2, ROWS, quarter), BF16),
        pltpu.VMEM((8, quarter), F32),
        pltpu.VMEM((8, quarter), F32),
        pltpu.VMEM((4, 8, HEAD), F32),
        pltpu.VMEM((4, 8, HEAD), F32),
        pltpu.VMEM((rows, tok), F32),
        dma((5,)), dma((2,)), dma((2,)), dma((2,)),
        dma((4,)), dma((4,)), dma((2, 2)), dma((2, 2)), dma((2,)), dma((2,)),
        dma((2,)), dma, dma,
        dma((3, 2)), dma((2, 2)), dma((4, 2)),
        dma((4, 2, 2)), dma((4, 2, 2)), dma((4, 2)), dma((4, 2)),
        dma((4,)), dma((4,)), dma((4, 3)), dma((4, 3)),
        dma((2, 4)), dma((2, 4)), dma((2, 4)), dma((2, 4)), dma((2, 4)), dma((2, 4)),
        dma((4,)), dma((4, 2)), dma, dma,
        dma((3,)), dma((3,)), dma((3,)), dma((3,)),
    ]
    grad, gain_key, gain_query = pl.pallas_call(
        kernel,
        name="image_row_gradients",
        out_shape=(
            jax.ShapeDtypeStruct((8, quarter), BF16),
            jax.ShapeDtypeStruct((1, HEAD), F32),
            jax.ShapeDtypeStruct((1, HEAD), F32),
        ),
        in_specs=[hbm] * 9,
        out_specs=(vmem, vmem, vmem),
        scratch_shapes=scratch,
        compiler_params=pltpu.CompilerParams(
            collective_id=0, has_side_effects=True, vmem_limit_bytes=62 * 1024 * 1024
        ),
    )(
        image_rows[0], key_weight[0], value_weight[0], key_gain, query_gain,
        queries[0, 0], cotangent[0, 0], text_doc, row_doc,
    )
    anywhere = pl.BlockSpec(memory_space=pl.ANY)
    return pl.pallas_call(
        hand_over,
        name="hand_over",
        out_shape=(
            jax.ShapeDtypeStruct((1, 8, quarter), BF16),
            jax.ShapeDtypeStruct((1, HEAD), F32),
            jax.ShapeDtypeStruct((1, HEAD), F32),
        ),
        in_specs=[anywhere] * 3,
        out_specs=(anywhere,) * 3,
        scratch_shapes=[dma((3,))],
        compiler_params=pltpu.CompilerParams(vmem_limit_bytes=62 * 1024 * 1024),
    )(grad[None], gain_key, gain_query)


def solution(mesh):
    in_specs = (
        P("dp", "section", None),
        P("section", None, "tensor"),
        P("section", None, "tensor"),
        P(),
        P(),
        P("dp", "section", None, "tensor"),
        P("dp", "section", None, "tensor"),
        P("dp", None),
        P("dp", None),
    )
    out_specs = (P("dp", "section", "tensor"), P("section", None), P("section", None))
    return jax.shard_map(
        on_device, mesh=mesh, in_specs=in_specs, out_specs=out_specs, check_vma=False
    )
```

```python
import math

import jax
import jax.numpy as jnp
from jax import lax
from jax.experimental import pallas as pl
from jax.experimental.pallas import tpu as pltpu
from jax.sharding import PartitionSpec as P

HEAD = 128
EPSILON = 1e-05
MESH = pl.DeviceIdType.MESH
F32 = jnp.float32
BF16 = jnp.bfloat16
ROWS = 16


def kernel(
    x_hbm, kw_ref, vw_ref, kg_hbm, qg_hbm, q_hbm, ct_hbm, td_hbm, rd_hbm,
    out_ref, gk_out, gq_out,
    x_ref, kg_ref, qg_ref, td_ref, rd_ref,
    wb, wm, q_buf, ct_buf, qs_buf, qn_buf, xs, xr,
    e_buf, g_buf, gs_buf, sums, kn_buf, ks_buf, key_buf, g, raw, raw_send, raw_recv, kv, p,
    y1, y2, ysum, yred, zin, fs, fr, gain_a, gain_b, mask,
    s_sem, w_sem, w_ss, w_rs, wz_ss, wz_rs, wx_ss, wx_rs, wf_ss, wf_rs, qc_sem, x_ss, x_rs, zo_ss, zf_ss, z_rs, ys_ss, y_rs, yf_ss, yf_rs,
    pr_ss, pr_rs, kv_ss, kv_rs, r1_ss, r1_rs, r2_ss, r2_rs, r3_ss, r3_rs,
    in_ss, in_rs, f_ss, f_rs, ga_ss, ga_rs, gb_ss, gb_rs,
):
    s = lax.axis_index("section")
    l = lax.axis_index("tensor")
    xi = lax.axis_index("dp")
    a = s // 8
    y = (s // 2) % 4
    c = s % 2
    half = g.shape[1]
    quarter = half // 2
    heads = q_hbm.shape[1] // HEAD
    tok = q_hbm.shape[0]
    group_cols = 2 * tok
    rows = g.shape[0]
    block = 4 * ROWS
    layer = s // 2

    def dev(a_=None, y_=None, c_=None, l_=None, x_=None):
        a_ = a if a_ is None else lax.rem(a_ + 8, 4)
        y_ = y if y_ is None else lax.rem(y_ + 8, 4)
        c_ = c if c_ is None else c_
        return {
            "section": (a_ * 4 + y_) * 2 + c_,
            "tensor": l if l_ is None else l_,
            "dp": xi if x_ is None else x_,
        }

    def remote(src, dst, ss, rs, to):
        return pltpu.make_async_remote_copy(
            src_ref=src, dst_ref=dst, send_sem=ss, recv_sem=rs, device_id=to, device_id_type=MESH
        )

    partner = dev(c_=1 - c)
    edge = jnp.logical_or(l == 0, l == 3)
    even = lax.rem(l, 2) == 0
    mate = jnp.where(even, l + 1, l - 1)
    step = jnp.where(even, 1, -1)
    a_of = [a, lax.rem(a - step + 4, 4), lax.rem(a + step + 4, 4), lax.rem(a + 2, 4)]

    small = [
        pltpu.make_async_copy(src, dst, s_sem.at[i])
        for i, (src, dst) in enumerate(
            [(x_hbm, x_ref), (kg_hbm, kg_ref), (qg_hbm, qg_ref), (td_hbm, td_ref), (rd_hbm, rd_ref)]
        )
    ]
    for copy in small:
        copy.start()

    barrier = pltpu.get_barrier_semaphore()

    def greet(to):
        pl.semaphore_signal(barrier, inc=1, device_id=to, device_id_type=MESH)

    greet(partner)
    greet(dev(y_=y + 1))
    greet(dev(y_=y - 1))
    for d in range(1, 4):
        greet(dev(l_=lax.rem(l + d, 4)))
        greet(dev(x_=lax.rem(xi + d, 4)))

    greet(dev(l_=mate, c_=1 - c))
    greet(dev(a_=a - step, l_=jnp.where(even, 3, 0)))

    own_rows = pl.ds(pl.multiple_of(c * half, 128), half)
    their_rows = pl.ds(pl.multiple_of((1 - c) * half, 128), half)
    loads = [
        pltpu.make_async_copy(kw_ref.at[own_rows, :], wb.at[:, 0:HEAD], w_sem.at[0]),
        pltpu.make_async_copy(vw_ref.at[own_rows, :], wb.at[:, HEAD : 2 * HEAD], w_sem.at[1]),
    ]
    for h in range(heads):
        for i, (src, dst) in enumerate(((q_hbm, q_buf), (ct_hbm, ct_buf))):
            there = dst.at[h * tok : (h + 1) * tok, :]
            loads.append(
                pltpu.make_async_copy(src.at[:, h * HEAD : (h + 1) * HEAD], there, qc_sem.at[i, h])
            )
    for copy in loads:
        copy.start()
    for copy in small:
        copy.wait()
    low = x_ref[:, :half].astype(F32)
    high = x_ref[:, half:].astype(F32)
    first = c == 0
    own = jnp.where(first, low, high)
    xs[...] = jnp.where(first, high, low)
    pl.semaphore_wait(barrier, 10 + jnp.where(edge, 2, 0))

    pending = []

    def send(copy, when=None):
        pending.append((when, copy))
        if when is None:
            copy.start()
        else:
            pl.when(when)(copy.start)

    share = quarter // 4

    def to_mate(i):
        core = c if i == 0 else 1 - c
        start = (2 * core + lax.rem(mate, 2)) * quarter + xi * share
        src_rows = pl.ds(pl.multiple_of(start, ROWS), share)
        dst_rows = pl.ds(pl.multiple_of(xi * share, ROWS), share)
        for j, ref in enumerate((kw_ref, vw_ref)):
            n = 2 * i + j
            dst = wm.at[dst_rows, n * HEAD : (n + 1) * HEAD]
            send(remote(ref.at[src_rows, :], dst, wz_ss.at[n], wz_rs.at[n], dev(l_=mate, c_=core)))

    def piece_of(x_, i):
        at = pl.ds(pl.multiple_of(lax.rem(x_ + 4, 4) * share, ROWS), share)
        return wm.at[at, 2 * i * HEAD : 2 * (i + 1) * HEAD]

    x_up, x_down = dev(x_=lax.rem(xi + 1, 4)), dev(x_=lax.rem(xi + 3, 4))

    def to_dp(i):
        for n in (2 * i, 2 * i + 1):
            at = pl.ds(pl.multiple_of(xi * share, ROWS), share)
            dst = wm.at[at, n * HEAD : (n + 1) * HEAD]
            remote(dst, dst, wz_ss.at[n], wz_rs.at[n], partner).wait_recv()
        own_piece = piece_of(xi, i)
        send(remote(own_piece, own_piece, wx_ss.at[i, 0], wx_rs.at[i, 0], x_up))
        send(remote(own_piece, own_piece, wx_ss.at[i, 1], wx_rs.at[i, 1], x_down))

    def dp_wait(i, side):
        part_ = piece_of(xi - 1 if side == 0 else xi + 1, i)
        remote(part_, part_, wx_ss.at[i, side], wx_rs.at[i, side], partner).wait_recv()

    def dp_forward(i):
        dp_wait(i, i)
        part_ = piece_of(xi - 1 if i == 0 else xi + 1, i)
        send(remote(part_, part_, wf_ss.at[i], wf_rs.at[i], x_up if i == 0 else x_down))

    def dp_finish():
        for i in range(2):
            dp_wait(i, 1 - i)
            part_ = piece_of(xi + 2, i)
            remote(part_, part_, wf_ss.at[i], wf_rs.at[i], partner).wait_recv()

    to_mate(0)
    send(remote(xs, xr, x_ss, x_rs, partner))
    x_copy = pending[-1][1]
    x_copy.wait_recv()
    got = xr[...]
    mine = pl.ds(pl.multiple_of((a * 4 + y) * ROWS, ROWS), ROWS)
    g[mine, :] = jnp.concatenate(
        [jnp.where(first, own, got), jnp.where(first, got, own)], axis=0
    ).astype(BF16)

    def shard(a_, y_, h):
        y_ = lax.rem(y_ + 8, 4)
        at = pl.ds(pl.multiple_of((a_ * 4 + y_) * ROWS, ROWS), ROWS)
        return g.at[at, h * quarter : (h + 1) * quarter]

    def y_send(k, h):
        piece = shard(a_of[k], y, h)
        send(remote(piece, piece, ys_ss.at[k, h, 0], y_rs.at[k, h, 0], dev(y_=y + 1)))
        send(remote(piece, piece, ys_ss.at[k, h, 1], y_rs.at[k, h, 1], dev(y_=y - 1)))

    def y_wait(k, h, side):
        piece = shard(a_of[k], y - 1 if side == 0 else y + 1, h)
        remote(piece, piece, ys_ss.at[k, h, side], y_rs.at[k, h, side], partner).wait_recv()

    def y_forward(k):
        for side in range(2):
            y_wait(k, side, side)
            piece = shard(a_of[k], y - 1 if side == 0 else y + 1, side)
            to = dev(y_=y + 1 if side == 0 else y - 1)
            send(remote(piece, piece, yf_ss.at[k, side], yf_rs.at[k, side], to))

    def y_finish(k):
        for side in range(2):
            y_wait(k, 1 - side, side)
        for side in range(2):
            piece = shard(a_of[k], y + 2, side)
            remote(piece, piece, yf_ss.at[k, side], yf_rs.at[k, side], partner).wait_recv()

    def z_wait(k, h):
        piece = shard(a_of[k], y, h)
        remote(piece, piece, zf_ss.at[0, h], z_rs.at[k, h], partner).wait_recv()

    last = l == 3
    far = jnp.where(last, 0, 3)
    side_a = jnp.where(last, a + 1, a - 1)
    beyond = dev(a_=side_a, l_=far)
    targets = [(beyond, 1), (dev(a_=side_a, l_=jnp.where(last, 2, 1)), 1)]
    for h in range(2):
        piece = shard(a, y, h)
        to, k = targets[0]
        send(remote(piece, piece, zo_ss.at[0, h], z_rs.at[k, h], to), edge)
        y_send(0, h)
    for h in range(2):
        piece = shard(a, y, h)
        to, k = targets[1]
        send(remote(piece, piece, zo_ss.at[1, h], z_rs.at[k, h], to), edge)
    send(remote(kw_ref.at[their_rows, :], wb.at[:, 2 * HEAD : 3 * HEAD], w_ss.at[0], w_rs.at[0], partner))
    send(remote(vw_ref.at[their_rows, :], wb.at[:, 3 * HEAD : 4 * HEAD], w_ss.at[1], w_rs.at[1], partner))
    w_copies = [pending[-2][1], pending[-1][1]]
    to_mate(1)

    for copy in loads[2:]:
        copy.wait()
    q_gain = qg_ref[pl.ds(layer, 1), :]
    k_gain = kg_ref[pl.ds(layer, 1), :]

    def norm_queries(h, carry):
        at = pl.ds(pl.multiple_of(h * tok, tok), tok)
        raw_q = q_buf[at, :].astype(F32)
        scale = lax.rsqrt(jnp.mean(raw_q * raw_q, axis=-1, keepdims=True) + EPSILON)
        normed = raw_q * scale
        qn_buf[at, :] = normed
        qs_buf[at, :] = (normed * q_gain).astype(BF16)
        return carry

    lax.fori_loop(0, heads, norm_queries, 0)
    row_doc = jnp.broadcast_to(rd_ref[...].astype(F32), (rows, rows)).T
    allowed = jnp.where(row_doc == td_ref[...].astype(F32), 1.0, 0.0)
    mask[:, :tok] = allowed
    mask[:, tok:] = allowed

    y_forward(0)
    for h in range(2):
        z_wait(1, h)
        piece = shard(a_of[1], y, h)
        send(remote(piece, piece, zf_ss.at[0, h], z_rs.at[2, h], dev(l_=mate)))
        y_send(1, h)

    def project(k):
        y_finish(k)
        at = pl.ds(pl.multiple_of(a_of[k] * block, block), block)
        out = jnp.dot(g[at, :], wb[...], preferred_element_type=F32)
        raw[at, :] = out[:, : 2 * HEAD]
        raw_send[at, :] = out[:, 2 * HEAD :]
        send(remote(raw_send.at[at, :], raw_recv.at[at, :], pr_ss.at[k], pr_rs.at[k], partner))

    factor = 1.0 / math.sqrt(HEAD)
    nt = (((1,), (1,)), ((), ()))
    tn = (((0,), (0,)), ((), ()))
    groups = range(0, heads * tok, group_cols)

    def scores_of(k):
        at = pl.ds(pl.multiple_of(a_of[k] * block, block), block)
        remote(raw_send.at[at, :], raw_recv.at[at, :], pr_ss.at[k], pr_rs.at[k], partner).wait_recv()
        projected = raw[at, :] + raw_recv[at, :]
        key_raw = projected[:, :HEAD]
        values = projected[:, HEAD:].astype(BF16)
        key_scale = lax.rsqrt(jnp.mean(key_raw * key_raw, axis=-1, keepdims=True) + EPSILON)
        key_normed = key_raw * key_scale
        keys = (key_normed * k_gain).astype(BF16)
        ks_buf[at, :] = jnp.broadcast_to(key_scale, key_raw.shape)
        kn_buf[at, :] = key_normed
        key_buf[at, :] = keys
        for start in groups:
            here = slice(start, start + group_cols)
            scores = lax.dot_general(keys, qs_buf[here, :], nt, preferred_element_type=F32)
            exponents = jnp.exp(scores * factor) * mask[at, :]
            grad_softmax = lax.dot_general(values, ct_buf[here, :], nt, preferred_element_type=F32)
            e_buf[at, here] = exponents
            g_buf[at, here] = grad_softmax
            total = jnp.sum(exponents, axis=0, keepdims=True)
            inner = jnp.sum(exponents * grad_softmax, axis=0, keepdims=True)
            if k > 0:
                total = total + sums[0:1, here]
                inner = inner + sums[1:2, here]
            if k == 3:
                total = 1.0 / total
                inner = inner * total
            sums[0:1, here] = total
            sums[1:2, here] = inner

    to_dp(0)
    loads[0].wait()
    loads[1].wait()
    for copy in w_copies:
        copy.wait_recv()
    project(0)
    for h in range(2):
        z_wait(2, h)
        piece = shard(a_of[2], y, h)
        send(remote(piece, piece, zo_ss.at[2, h], z_rs.at[3, h], beyond), edge)
        y_send(2, h)
    y_forward(1)
    to_dp(1)
    for h in range(2):
        z_wait(3, h)
        piece = shard(a_of[3], y, h)
        send(remote(piece, piece, zf_ss.at[1, h], z_rs.at[3, h], dev(l_=mate)), edge)
        y_send(3, h)
    y_forward(2)
    dp_forward(0)
    project(1)
    scores_of(0)
    y_forward(3)
    dp_forward(1)
    scores_of(1)
    project(2)
    scores_of(2)
    project(3)
    scores_of(3)

    b_of = [lax.rem(a + 2, 4), lax.rem(a + 1, 4), lax.rem(a + 3, 4), a]
    kv_to = [partner, dev(l_=mate), dev(l_=mate, c_=1 - c)]

    def kv_copy(k, i):
        at = pl.ds(pl.multiple_of(b_of[k] * block, block), block)
        dst = kv.at[at, 2 * (i + 1) * HEAD : 2 * (i + 2) * HEAD]
        return remote(kv.at[at, : 2 * HEAD], dst, kv_ss.at[k, i], kv_rs.at[k, i], kv_to[i])

    key_gains = []

    def grads():
        at = slice(0, rows)
        grad_key = jnp.zeros((rows, HEAD), F32)
        grad_value = jnp.zeros((rows, HEAD), F32)
        for start in groups:
            here = slice(start, start + group_cols)
            softmax = e_buf[at, here] * sums[0:1, here]
            grad_scores = (softmax * (g_buf[at, here] - sums[1:2, here])).astype(BF16)
            gs_buf[at, here] = grad_scores
            grad_value += jnp.dot(softmax.astype(BF16), ct_buf[here, :], preferred_element_type=F32)
            grad_key += jnp.dot(grad_scores, qs_buf[here, :], preferred_element_type=F32)
        grad_key = grad_key * factor
        key_normed = kn_buf[at, :]
        scaled_up = grad_key * k_gain
        key_back = ks_buf[at, :] * (
            scaled_up - key_normed * jnp.mean(scaled_up * key_normed, axis=-1, keepdims=True)
        )
        kv[at, :HEAD] = key_back.astype(BF16)
        kv[at, HEAD : 2 * HEAD] = grad_value.astype(BF16)
        for k in range(4):
            for i in range(3):
                send(kv_copy(k, i))
        key_gains.append(jnp.sum(grad_key * key_normed, axis=0, keepdims=True))

    def share_gains():
        gain_query = jnp.zeros((1, HEAD), F32)
        for start in groups:
            here = slice(start, start + group_cols)
            grad_query = lax.dot_general(gs_buf[:, here], key_buf[...], tn, preferred_element_type=F32)
            gain_query += jnp.sum(grad_query * qn_buf[here, :], axis=0, keepdims=True)
        gain_a[l] = jnp.concatenate(
            [sum(key_gains), gain_query * factor, jnp.zeros((6, HEAD), F32)], axis=0
        )
        for d in range(1, 4):
            to = dev(l_=lax.rem(l + d, 4))
            send(remote(gain_a.at[l], gain_a.at[l], ga_ss.at[d - 1], ga_rs.at[d - 1], to))

    y_up, y_down = dev(y_=y + 1), dev(y_=y - 1)
    split = quarter // 2 // HEAD * HEAD + HEAD
    cols = [slice(0, split), slice(split, quarter)]
    width = [split, quarter - split]
    w_rows = pl.ds(pl.multiple_of(lax.rem(l, 2) * quarter, ROWS), quarter)

    def part(b, y_, h=None):
        y_ = lax.rem(y_ + 8, 4)
        at = pl.ds(pl.multiple_of((b * 4 + y_) * ROWS, ROWS), ROWS)
        return p.at[at, :] if h is None else p.at[at, cols[h]]

    def y1_at(h, k):
        return y1.at[h, k, :, : width[h]]

    def terms(k):
        for i in range(3):
            kv_copy(k, i).wait_recv()
        at = pl.ds(pl.multiple_of(b_of[k] * block, block), block)
        p[at, :] = (
            lax.dot_general(kv[at, : 4 * HEAD], wb[w_rows, :], nt, preferred_element_type=F32)
            + lax.dot_general(kv[at, 4 * HEAD :], wm[...], nt, preferred_element_type=F32)
        ).astype(BF16)

    def opposite(k):
        b = b_of[k]
        for h in range(2):
            send(remote(part(b, y + 2, h), y1_at(h, k), r1_ss.at[h, k], r1_rs.at[h, k], y_up if h == 0 else y_down))

    def beside(k):
        b = b_of[k]
        for h in range(2):
            src = part(b, y + 1, 1) if h == 0 else part(b, y - 1, 0)
            dst = y2.at[h, k, :, cols[1 - h]]
            send(remote(src, dst, r2_ss.at[h, k], r2_rs.at[h, k], y_up if h == 0 else y_down))

    def pass_on(k):
        b = b_of[k]
        for h in range(2):
            remote(y1_at(h, k), y1_at(h, k), r1_ss.at[h, k], r1_rs.at[h, k], partner).wait_recv()
            mine_ = part(b, y + 1, 0) if h == 0 else part(b, y - 1, 1)
            total = ysum.at[h, k, :, : width[h]]
            total[...] = (mine_[...].astype(F32) + y1_at(h, k)[...].astype(F32)).astype(BF16)
            send(remote(total, y2.at[h, k, :, cols[h]], r3_ss.at[h, k], r3_rs.at[h, k], y_up if h == 0 else y_down))

    active = c == l // 2

    owner = jnp.where(active, l, lax.rem(l + 2, 4))
    slot = jnp.where(active, 0, 1)

    def group(k):
        b = b_of[k]
        for h in range(2):
            for sem_s, sem_r, i in ((r2_ss, r2_rs, 1 - h), (r3_ss, r3_rs, h)):
                dst = y2.at[h, k, :, cols[i]]
                remote(dst, dst, sem_s.at[h, k], sem_r.at[h, k], partner).wait_recv()
        total = part(b, y)[...].astype(F32) + y2[0, k].astype(F32) + y2[1, k].astype(F32)
        yred[k] = total.astype(BF16)
        to = dev(a_=b, l_=owner)
        copy = remote(yred.at[k], zin.at[k, slot], in_ss.at[k], in_rs.at[k, slot], to)
        send(copy, jnp.logical_not(active) if k == 3 else None)

    grads()
    share_gains()
    dp_finish()
    terms(0)
    opposite(0)
    beside(0)
    terms(1)
    opposite(1)
    pass_on(0)
    beside(1)
    terms(2)
    opposite(2)
    pass_on(1)
    beside(2)
    terms(3)
    opposite(3)
    for d in range(1, 4):
        src = gain_a.at[lax.rem(l - d + 4, 4)]
        remote(src, src, ga_ss.at[d - 1], ga_rs.at[d - 1], partner).wait_recv()
    gain_b[xi] = gain_a[0] + gain_a[1] + gain_a[2] + gain_a[3]
    for d in range(1, 4):
        to = dev(x_=lax.rem(xi + d, 4))
        send(remote(gain_b.at[xi], gain_b.at[xi], gb_ss.at[d - 1], gb_rs.at[d - 1], to))

    group(0)
    pass_on(2)
    beside(3)
    group(1)
    pass_on(3)
    group(2)
    group(3)

    for d in range(1, 4):
        src = gain_b.at[lax.rem(xi - d + 4, 4)]
        remote(src, src, gb_ss.at[d - 1], gb_rs.at[d - 1], partner).wait_recv()
    gains = gain_b[0] + gain_b[1] + gain_b[2] + gain_b[3]
    gk_out[...] = gains[0:1]
    gq_out[...] = gains[1:2]

    f_copy = remote(fs, fr, f_ss, f_rs, partner)

    @pl.when(active)
    def _():
        total = yred[3].astype(F32)
        for k in range(4):
            for j in range(1 if k == 3 else 0, 2):
                got_ = zin.at[k, j]
                remote(got_, got_, in_ss.at[k], in_rs.at[k, j], partner).wait_recv()
                total = total + got_[...].astype(F32)
        top, bottom = total[: ROWS // 2], total[ROWS // 2 :]
        fs[...] = jnp.where(first, bottom, top)
        f_copy.start()
        out_ref[...] = jnp.where(first, top, bottom).astype(BF16)
        f_copy.wait_send()

    @pl.when(jnp.logical_not(active))
    def _():
        f_copy.wait_recv()
        out_ref[...] = fr[...].astype(BF16)

    for when, copy in pending:
        if when is None:
            copy.wait_send()
        else:
            pl.when(when)(copy.wait_send)


def hand_over(a_ref, b_ref, c_ref, a_out, b_out, c_out, sems):
    copies = [
        pltpu.make_async_copy(src, dst, sems.at[i])
        for i, (src, dst) in enumerate([(a_ref, a_out), (b_ref, b_out), (c_ref, c_out)])
    ]
    for copy in copies:
        copy.start()
    for copy in copies:
        copy.wait()


def on_device(
    image_rows,
    key_weight,
    value_weight,
    key_gain,
    query_gain,
    queries,
    cotangent,
    text_doc,
    row_doc,
):
    width = image_rows.shape[2]
    half = width // 2
    quarter = half // 2
    tok = queries.shape[2]
    q_width = queries.shape[3]
    rows = row_doc.shape[1]
    vmem = pl.BlockSpec(memory_space=pltpu.VMEM)
    hbm = pl.BlockSpec(memory_space=pltpu.HBM)
    dma = pltpu.SemaphoreType.DMA
    stacked = tok * q_width // HEAD
    scratch = [
        pltpu.VMEM((8, width), BF16),
        pltpu.VMEM(key_gain.shape, F32),
        pltpu.VMEM(query_gain.shape, F32),
        pltpu.VMEM(text_doc.shape, jnp.int32),
        pltpu.VMEM(row_doc.shape, jnp.int32),
        pltpu.VMEM((half, 4 * HEAD), BF16),
        pltpu.VMEM((quarter, 4 * HEAD), BF16),
        pltpu.VMEM((stacked, HEAD), BF16),
        pltpu.VMEM((stacked, HEAD), BF16),
        pltpu.VMEM((stacked, HEAD), BF16),
        pltpu.VMEM((stacked, HEAD), F32),
        pltpu.VMEM((8, half), F32),
        pltpu.VMEM((8, half), F32),
        pltpu.VMEM((rows, stacked), F32),
        pltpu.VMEM((rows, stacked), F32),
        pltpu.VMEM((rows, stacked), BF16),
        pltpu.VMEM((8, stacked), F32),
        pltpu.VMEM((rows, HEAD), F32),
        pltpu.VMEM((rows, HEAD), F32),
        pltpu.VMEM((rows, HEAD), BF16),
        pltpu.VMEM((rows, half), BF16),
        pltpu.VMEM((rows, 2 * HEAD), F32),
        pltpu.VMEM((rows, 2 * HEAD), F32),
        pltpu.VMEM((rows, 2 * HEAD), F32),
        pltpu.VMEM((rows, 8 * HEAD), BF16),
        pltpu.VMEM((rows, quarter), BF16),
        pltpu.VMEM((2, 4, ROWS, quarter), BF16),
        pltpu.VMEM((2, 4, ROWS, quarter), BF16),
        pltpu.VMEM((2, 4, ROWS, quarter), BF16),
        pltpu.VMEM((4, ROWS, quarter), BF16),
        pltpu.VMEM((4, 2, ROWS, quarter), BF16),
        pltpu.VMEM((8, quarter), F32),
        pltpu.VMEM((8, quarter), F32),
        pltpu.VMEM((4, 8, HEAD), F32),
        pltpu.VMEM((4, 8, HEAD), F32),
        pltpu.VMEM((rows, 2 * tok), F32),
        dma((5,)), dma((2,)), dma((2,)), dma((2,)),
        dma((4,)), dma((4,)), dma((2, 2)), dma((2, 2)), dma((2,)), dma((2,)),
        dma((2, q_width // HEAD)), dma, dma,
        dma((3, 2)), dma((2, 2)), dma((4, 2)),
        dma((4, 2, 2)), dma((4, 2, 2)), dma((4, 2)), dma((4, 2)),
        dma((4,)), dma((4,)), dma((4, 3)), dma((4, 3)),
        dma((2, 4)), dma((2, 4)), dma((2, 4)), dma((2, 4)), dma((2, 4)), dma((2, 4)),
        dma((4,)), dma((4, 2)), dma, dma,
        dma((3,)), dma((3,)), dma((3,)), dma((3,)),
    ]
    grad, gain_key, gain_query = pl.pallas_call(
        kernel,
        name="image_row_gradients",
        out_shape=(
            jax.ShapeDtypeStruct((8, quarter), BF16),
            jax.ShapeDtypeStruct((1, HEAD), F32),
            jax.ShapeDtypeStruct((1, HEAD), F32),
        ),
        in_specs=[hbm] * 9,
        out_specs=(vmem, vmem, vmem),
        scratch_shapes=scratch,
        compiler_params=pltpu.CompilerParams(
            collective_id=0, has_side_effects=True, vmem_limit_bytes=62 * 1024 * 1024
        ),
    )(
        image_rows[0], key_weight[0], value_weight[0], key_gain, query_gain,
        queries[0, 0], cotangent[0, 0], text_doc, row_doc,
    )
    anywhere = pl.BlockSpec(memory_space=pl.ANY)
    return pl.pallas_call(
        hand_over,
        name="hand_over",
        out_shape=(
            jax.ShapeDtypeStruct((1, 8, quarter), BF16),
            jax.ShapeDtypeStruct((1, HEAD), F32),
            jax.ShapeDtypeStruct((1, HEAD), F32),
        ),
        in_specs=[anywhere] * 3,
        out_specs=(anywhere,) * 3,
        scratch_shapes=[dma((3,))],
        compiler_params=pltpu.CompilerParams(vmem_limit_bytes=62 * 1024 * 1024),
    )(grad[None], gain_key, gain_query)


def solution(mesh):
    in_specs = (
        P("dp", "section", None),
        P("section", None, "tensor"),
        P("section", None, "tensor"),
        P(),
        P(),
        P("dp", "section", None, "tensor"),
        P("dp", "section", None, "tensor"),
        P("dp", None),
        P("dp", None),
    )
    out_specs = (P("dp", "section", "tensor"), P("section", None), P("section", None))
    return jax.shard_map(
        on_device, mesh=mesh, in_specs=in_specs, out_specs=out_specs, check_vma=False
    )
```

```python
import math

import jax
import jax.numpy as jnp
from jax import lax
from jax.experimental import pallas as pl
from jax.experimental.pallas import tpu as pltpu
from jax.sharding import PartitionSpec as P

HEAD = 128
EPSILON = 1e-05
MESH = pl.DeviceIdType.MESH
F32 = jnp.float32
BF16 = jnp.bfloat16
ROWS = 16


def kernel(
    x_hbm, kw_ref, vw_ref, kg_hbm, qg_hbm, q_hbm, ct_hbm, td_hbm, rd_hbm,
    out_ref, gk_out, gq_out,
    x_ref, kg_ref, qg_ref, td_ref, rd_ref,
    wb, wm, q_buf, ct_buf, qs_buf, qn_buf, xs, xr,
    e_buf, g_buf, gs_buf, sums, kn_buf, ks_buf, key_buf, g, raw, raw_send, raw_recv, kv, p,
    y1, y2, ysum, yred, zin, fs, fr, gain_a, gain_b, mask,
    s_sem, w_sem, w_ss, w_rs, wz_ss, wz_rs, wx_ss, wx_rs, wf_ss, wf_rs, qc_sem, x_ss, x_rs, zo_ss, zf_ss, z_rs, ys_ss, y_rs, yf_ss, yf_rs,
    pr_ss, pr_rs, kv_ss, kv_rs, r1_ss, r1_rs, r2_ss, r2_rs, r3_ss, r3_rs,
    in_ss, in_rs, f_ss, f_rs, ga_ss, ga_rs, gb_ss, gb_rs,
):
    s = lax.axis_index("section")
    l = lax.axis_index("tensor")
    xi = lax.axis_index("dp")
    a = s // 8
    y = (s // 2) % 4
    c = s % 2
    half = g.shape[1]
    quarter = half // 2
    heads = q_hbm.shape[1] // HEAD
    tok = q_hbm.shape[0]
    group_cols = 2 * tok
    rows = g.shape[0]
    block = 4 * ROWS
    layer = s // 2

    def dev(a_=None, y_=None, c_=None, l_=None, x_=None):
        a_ = a if a_ is None else lax.rem(a_ + 8, 4)
        y_ = y if y_ is None else lax.rem(y_ + 8, 4)
        c_ = c if c_ is None else c_
        return {
            "section": (a_ * 4 + y_) * 2 + c_,
            "tensor": l if l_ is None else l_,
            "dp": xi if x_ is None else x_,
        }

    def remote(src, dst, ss, rs, to):
        return pltpu.make_async_remote_copy(
            src_ref=src, dst_ref=dst, send_sem=ss, recv_sem=rs, device_id=to, device_id_type=MESH
        )

    partner = dev(c_=1 - c)
    edge = jnp.logical_or(l == 0, l == 3)
    even = lax.rem(l, 2) == 0
    mate = jnp.where(even, l + 1, l - 1)
    step = jnp.where(even, 1, -1)
    a_of = [a, lax.rem(a - step + 4, 4), lax.rem(a + step + 4, 4), lax.rem(a + 2, 4)]

    barrier = pltpu.get_barrier_semaphore()

    def greet(to):
        pl.semaphore_signal(barrier, inc=1, device_id=to, device_id_type=MESH)

    greet(partner)
    greet(dev(y_=y + 1))
    greet(dev(y_=y - 1))
    for d in range(1, 4):
        greet(dev(l_=lax.rem(l + d, 4)))
        greet(dev(x_=lax.rem(xi + d, 4)))

    greet(dev(l_=mate, c_=1 - c))
    greet(dev(a_=a - step, l_=jnp.where(even, 3, 0)))

    small = [
        pltpu.make_async_copy(src, dst, s_sem.at[i])
        for i, (src, dst) in enumerate(
            [(x_hbm, x_ref), (kg_hbm, kg_ref), (qg_hbm, qg_ref), (td_hbm, td_ref), (rd_hbm, rd_ref)]
        )
    ]
    for copy in small:
        copy.start()

    own_rows = pl.ds(pl.multiple_of(c * half, 128), half)
    their_rows = pl.ds(pl.multiple_of((1 - c) * half, 128), half)
    loads = [
        pltpu.make_async_copy(kw_ref.at[own_rows, :], wb.at[:, 0:HEAD], w_sem.at[0]),
        pltpu.make_async_copy(vw_ref.at[own_rows, :], wb.at[:, HEAD : 2 * HEAD], w_sem.at[1]),
    ]
    for h in range(heads):
        for i, (src, dst) in enumerate(((q_hbm, q_buf), (ct_hbm, ct_buf))):
            there = dst.at[h * tok : (h + 1) * tok, :]
            loads.append(
                pltpu.make_async_copy(src.at[:, h * HEAD : (h + 1) * HEAD], there, qc_sem.at[i, h])
            )
    for copy in loads:
        copy.start()
    for copy in small:
        copy.wait()
    low = x_ref[:, :half].astype(F32)
    high = x_ref[:, half:].astype(F32)
    first = c == 0
    own = jnp.where(first, low, high)
    xs[...] = jnp.where(first, high, low)
    pl.semaphore_wait(barrier, 10 + jnp.where(edge, 2, 0))

    pending = []

    def send(copy, when=None):
        pending.append((when, copy))
        if when is None:
            copy.start()
        else:
            pl.when(when)(copy.start)

    share = quarter // 4

    def to_mate(i):
        core = c if i == 0 else 1 - c
        start = (2 * core + lax.rem(mate, 2)) * quarter + xi * share
        src_rows = pl.ds(pl.multiple_of(start, ROWS), share)
        dst_rows = pl.ds(pl.multiple_of(xi * share, ROWS), share)
        for j, ref in enumerate((kw_ref, vw_ref)):
            n = 2 * i + j
            dst = wm.at[dst_rows, n * HEAD : (n + 1) * HEAD]
            send(remote(ref.at[src_rows, :], dst, wz_ss.at[n], wz_rs.at[n], dev(l_=mate, c_=core)))

    def piece_of(x_, i):
        at = pl.ds(pl.multiple_of(lax.rem(x_ + 4, 4) * share, ROWS), share)
        return wm.at[at, 2 * i * HEAD : 2 * (i + 1) * HEAD]

    x_up, x_down = dev(x_=lax.rem(xi + 1, 4)), dev(x_=lax.rem(xi + 3, 4))

    def to_dp(i):
        for n in (2 * i, 2 * i + 1):
            at = pl.ds(pl.multiple_of(xi * share, ROWS), share)
            dst = wm.at[at, n * HEAD : (n + 1) * HEAD]
            remote(dst, dst, wz_ss.at[n], wz_rs.at[n], partner).wait_recv()
        own_piece = piece_of(xi, i)
        send(remote(own_piece, own_piece, wx_ss.at[i, 0], wx_rs.at[i, 0], x_up))
        send(remote(own_piece, own_piece, wx_ss.at[i, 1], wx_rs.at[i, 1], x_down))

    def dp_wait(i, side):
        part_ = piece_of(xi - 1 if side == 0 else xi + 1, i)
        remote(part_, part_, wx_ss.at[i, side], wx_rs.at[i, side], partner).wait_recv()

    def dp_forward(i):
        dp_wait(i, i)
        part_ = piece_of(xi - 1 if i == 0 else xi + 1, i)
        send(remote(part_, part_, wf_ss.at[i], wf_rs.at[i], x_up if i == 0 else x_down))

    def dp_finish():
        for i in range(2):
            dp_wait(i, 1 - i)
            part_ = piece_of(xi + 2, i)
            remote(part_, part_, wf_ss.at[i], wf_rs.at[i], partner).wait_recv()

    send(remote(xs, xr, x_ss, x_rs, partner))
    x_copy = pending[-1][1]
    to_mate(0)
    x_copy.wait_recv()
    got = xr[...]
    mine = pl.ds(pl.multiple_of((a * 4 + y) * ROWS, ROWS), ROWS)
    g[mine, :] = jnp.concatenate(
        [jnp.where(first, own, got), jnp.where(first, got, own)], axis=0
    ).astype(BF16)

    def shard(a_, y_, h):
        y_ = lax.rem(y_ + 8, 4)
        at = pl.ds(pl.multiple_of((a_ * 4 + y_) * ROWS, ROWS), ROWS)
        return g.at[at, h * quarter : (h + 1) * quarter]

    def y_send(k, h):
        piece = shard(a_of[k], y, h)
        send(remote(piece, piece, ys_ss.at[k, h, 0], y_rs.at[k, h, 0], dev(y_=y + 1)))
        send(remote(piece, piece, ys_ss.at[k, h, 1], y_rs.at[k, h, 1], dev(y_=y - 1)))

    def y_wait(k, h, side):
        piece = shard(a_of[k], y - 1 if side == 0 else y + 1, h)
        remote(piece, piece, ys_ss.at[k, h, side], y_rs.at[k, h, side], partner).wait_recv()

    def y_forward(k):
        for side in range(2):
            y_wait(k, side, side)
            piece = shard(a_of[k], y - 1 if side == 0 else y + 1, side)
            to = dev(y_=y + 1 if side == 0 else y - 1)
            send(remote(piece, piece, yf_ss.at[k, side], yf_rs.at[k, side], to))

    def y_finish(k):
        for side in range(2):
            y_wait(k, 1 - side, side)
        for side in range(2):
            piece = shard(a_of[k], y + 2, side)
            remote(piece, piece, yf_ss.at[k, side], yf_rs.at[k, side], partner).wait_recv()

    def z_wait(k, h):
        piece = shard(a_of[k], y, h)
        remote(piece, piece, zf_ss.at[0, h], z_rs.at[k, h], partner).wait_recv()

    last = l == 3
    far = jnp.where(last, 0, 3)
    side_a = jnp.where(last, a + 1, a - 1)
    beyond = dev(a_=side_a, l_=far)
    targets = [(beyond, 1), (dev(a_=side_a, l_=jnp.where(last, 2, 1)), 1)]
    for h in range(2):
        piece = shard(a, y, h)
        to, k = targets[0]
        send(remote(piece, piece, zo_ss.at[0, h], z_rs.at[k, h], to), edge)
        y_send(0, h)
    for h in range(2):
        piece = shard(a, y, h)
        to, k = targets[1]
        send(remote(piece, piece, zo_ss.at[1, h], z_rs.at[k, h], to), edge)
    send(remote(kw_ref.at[their_rows, :], wb.at[:, 2 * HEAD : 3 * HEAD], w_ss.at[0], w_rs.at[0], partner))
    send(remote(vw_ref.at[their_rows, :], wb.at[:, 3 * HEAD : 4 * HEAD], w_ss.at[1], w_rs.at[1], partner))
    w_copies = [pending[-2][1], pending[-1][1]]
    to_mate(1)

    for copy in loads[2:]:
        copy.wait()
    q_gain = qg_ref[pl.ds(layer, 1), :]
    k_gain = kg_ref[pl.ds(layer, 1), :]

    def norm_queries(h, carry):
        at = pl.ds(pl.multiple_of(h * tok, tok), tok)
        raw_q = q_buf[at, :].astype(F32)
        scale = lax.rsqrt(jnp.mean(raw_q * raw_q, axis=-1, keepdims=True) + EPSILON)
        normed = raw_q * scale
        qn_buf[at, :] = normed
        qs_buf[at, :] = (normed * q_gain).astype(BF16)
        return carry

    lax.fori_loop(0, heads, norm_queries, 0)
    row_doc = jnp.broadcast_to(rd_ref[...].astype(F32), (rows, rows)).T
    allowed = jnp.where(row_doc == td_ref[...].astype(F32), 1.0, 0.0)
    mask[:, :tok] = allowed
    mask[:, tok:] = allowed

    y_forward(0)
    for h in range(2):
        z_wait(1, h)
        piece = shard(a_of[1], y, h)
        send(remote(piece, piece, zf_ss.at[0, h], z_rs.at[2, h], dev(l_=mate)))
        y_send(1, h)

    def project(k):
        y_finish(k)
        at = pl.ds(pl.multiple_of(a_of[k] * block, block), block)
        out = jnp.dot(g[at, :], wb[...], preferred_element_type=F32)
        raw[at, :] = out[:, : 2 * HEAD]
        raw_send[at, :] = out[:, 2 * HEAD :]
        send(remote(raw_send.at[at, :], raw_recv.at[at, :], pr_ss.at[k], pr_rs.at[k], partner))

    factor = 1.0 / math.sqrt(HEAD)
    nt = (((1,), (1,)), ((), ()))
    tn = (((0,), (0,)), ((), ()))
    groups = range(0, heads * tok, group_cols)

    def scores_of(k):
        at = pl.ds(pl.multiple_of(a_of[k] * block, block), block)
        remote(raw_send.at[at, :], raw_recv.at[at, :], pr_ss.at[k], pr_rs.at[k], partner).wait_recv()
        projected = raw[at, :] + raw_recv[at, :]
        key_raw = projected[:, :HEAD]
        values = projected[:, HEAD:].astype(BF16)
        key_scale = lax.rsqrt(jnp.mean(key_raw * key_raw, axis=-1, keepdims=True) + EPSILON)
        key_normed = key_raw * key_scale
        keys = (key_normed * k_gain).astype(BF16)
        ks_buf[at, :] = jnp.broadcast_to(key_scale, key_raw.shape)
        kn_buf[at, :] = key_normed
        key_buf[at, :] = keys
        for start in groups:
            here = slice(start, start + group_cols)
            scores = lax.dot_general(keys, qs_buf[here, :], nt, preferred_element_type=F32)
            exponents = jnp.exp(scores * factor) * mask[at, :]
            grad_softmax = lax.dot_general(values, ct_buf[here, :], nt, preferred_element_type=F32)
            e_buf[at, here] = exponents
            g_buf[at, here] = grad_softmax
            total = jnp.sum(exponents, axis=0, keepdims=True)
            inner = jnp.sum(exponents * grad_softmax, axis=0, keepdims=True)
            if k > 0:
                total = total + sums[0:1, here]
                inner = inner + sums[1:2, here]
            if k == 3:
                total = 1.0 / total
                inner = inner * total
            sums[0:1, here] = total
            sums[1:2, here] = inner

    to_dp(0)
    loads[0].wait()
    loads[1].wait()
    for copy in w_copies:
        copy.wait_recv()
    project(0)
    for h in range(2):
        z_wait(2, h)
        piece = shard(a_of[2], y, h)
        send(remote(piece, piece, zo_ss.at[2, h], z_rs.at[3, h], beyond), edge)
        y_send(2, h)
    y_forward(1)
    to_dp(1)
    for h in range(2):
        z_wait(3, h)
        piece = shard(a_of[3], y, h)
        send(remote(piece, piece, zf_ss.at[1, h], z_rs.at[3, h], dev(l_=mate)), edge)
        y_send(3, h)
    y_forward(2)
    dp_forward(0)
    project(1)
    scores_of(0)
    y_forward(3)
    dp_forward(1)
    scores_of(1)
    project(2)
    scores_of(2)
    project(3)
    scores_of(3)

    b_of = [lax.rem(a + 2, 4), lax.rem(a + 1, 4), lax.rem(a + 3, 4), a]
    kv_to = [partner, dev(l_=mate), dev(l_=mate, c_=1 - c)]

    def kv_copy(k, i):
        at = pl.ds(pl.multiple_of(b_of[k] * block, block), block)
        dst = kv.at[at, 2 * (i + 1) * HEAD : 2 * (i + 2) * HEAD]
        return remote(kv.at[at, : 2 * HEAD], dst, kv_ss.at[k, i], kv_rs.at[k, i], kv_to[i])

    key_gains = []

    def grads():
        at = slice(0, rows)
        grad_key = jnp.zeros((rows, HEAD), F32)
        grad_value = jnp.zeros((rows, HEAD), F32)
        for start in groups:
            here = slice(start, start + group_cols)
            softmax = e_buf[at, here] * sums[0:1, here]
            grad_scores = (softmax * (g_buf[at, here] - sums[1:2, here])).astype(BF16)
            gs_buf[at, here] = grad_scores
            grad_value += jnp.dot(softmax.astype(BF16), ct_buf[here, :], preferred_element_type=F32)
            grad_key += jnp.dot(grad_scores, qs_buf[here, :], preferred_element_type=F32)
        grad_key = grad_key * factor
        key_normed = kn_buf[at, :]
        scaled_up = grad_key * k_gain
        key_back = ks_buf[at, :] * (
            scaled_up - key_normed * jnp.mean(scaled_up * key_normed, axis=-1, keepdims=True)
        )
        kv[at, :HEAD] = key_back.astype(BF16)
        kv[at, HEAD : 2 * HEAD] = grad_value.astype(BF16)
        for k in range(4):
            for i in range(3):
                send(kv_copy(k, i))
        key_gains.append(jnp.sum(grad_key * key_normed, axis=0, keepdims=True))

    def share_gains():
        gain_query = jnp.zeros((1, HEAD), F32)
        for start in groups:
            here = slice(start, start + group_cols)
            grad_query = lax.dot_general(gs_buf[:, here], key_buf[...], tn, preferred_element_type=F32)
            gain_query += jnp.sum(grad_query * qn_buf[here, :], axis=0, keepdims=True)
        gain_a[l] = jnp.concatenate(
            [sum(key_gains), gain_query * factor, jnp.zeros((6, HEAD), F32)], axis=0
        )
        for d in range(1, 4):
            to = dev(l_=lax.rem(l + d, 4))
            send(remote(gain_a.at[l], gain_a.at[l], ga_ss.at[d - 1], ga_rs.at[d - 1], to))

    y_up, y_down = dev(y_=y + 1), dev(y_=y - 1)
    split = quarter // 2 // HEAD * HEAD + HEAD
    cols = [slice(0, split), slice(split, quarter)]
    width = [split, quarter - split]
    w_rows = pl.ds(pl.multiple_of(lax.rem(l, 2) * quarter, ROWS), quarter)

    def part(b, y_, h=None):
        y_ = lax.rem(y_ + 8, 4)
        at = pl.ds(pl.multiple_of((b * 4 + y_) * ROWS, ROWS), ROWS)
        return p.at[at, :] if h is None else p.at[at, cols[h]]

    def y1_at(h, k):
        return y1.at[h, k, :, : width[h]]

    def terms(k):
        for i in range(3):
            kv_copy(k, i).wait_recv()
        at = pl.ds(pl.multiple_of(b_of[k] * block, block), block)
        p[at, :] = (
            lax.dot_general(kv[at, : 4 * HEAD], wb[w_rows, :], nt, preferred_element_type=F32)
            + lax.dot_general(kv[at, 4 * HEAD :], wm[...], nt, preferred_element_type=F32)
        ).astype(BF16)

    def opposite(k):
        b = b_of[k]
        for h in range(2):
            send(remote(part(b, y + 2, h), y1_at(h, k), r1_ss.at[h, k], r1_rs.at[h, k], y_up if h == 0 else y_down))

    def beside(k):
        b = b_of[k]
        for h in range(2):
            src = part(b, y + 1, 1) if h == 0 else part(b, y - 1, 0)
            dst = y2.at[h, k, :, cols[1 - h]]
            send(remote(src, dst, r2_ss.at[h, k], r2_rs.at[h, k], y_up if h == 0 else y_down))

    def pass_on(k):
        b = b_of[k]
        for h in range(2):
            remote(y1_at(h, k), y1_at(h, k), r1_ss.at[h, k], r1_rs.at[h, k], partner).wait_recv()
            mine_ = part(b, y + 1, 0) if h == 0 else part(b, y - 1, 1)
            total = ysum.at[h, k, :, : width[h]]
            total[...] = (mine_[...].astype(F32) + y1_at(h, k)[...].astype(F32)).astype(BF16)
            send(remote(total, y2.at[h, k, :, cols[h]], r3_ss.at[h, k], r3_rs.at[h, k], y_up if h == 0 else y_down))

    active = c == l // 2

    owner = jnp.where(active, l, lax.rem(l + 2, 4))
    slot = jnp.where(active, 0, 1)

    def group(k):
        b = b_of[k]
        for h in range(2):
            for sem_s, sem_r, i in ((r2_ss, r2_rs, 1 - h), (r3_ss, r3_rs, h)):
                dst = y2.at[h, k, :, cols[i]]
                remote(dst, dst, sem_s.at[h, k], sem_r.at[h, k], partner).wait_recv()
        total = part(b, y)[...].astype(F32) + y2[0, k].astype(F32) + y2[1, k].astype(F32)
        yred[k] = total.astype(BF16)
        to = dev(a_=b, l_=owner)
        copy = remote(yred.at[k], zin.at[k, slot], in_ss.at[k], in_rs.at[k, slot], to)
        send(copy, jnp.logical_not(active) if k == 3 else None)

    grads()
    share_gains()
    dp_finish()
    terms(0)
    opposite(0)
    beside(0)
    terms(1)
    opposite(1)
    pass_on(0)
    beside(1)
    terms(2)
    opposite(2)
    pass_on(1)
    beside(2)
    terms(3)
    opposite(3)
    for d in range(1, 4):
        src = gain_a.at[lax.rem(l - d + 4, 4)]
        remote(src, src, ga_ss.at[d - 1], ga_rs.at[d - 1], partner).wait_recv()
    gain_b[xi] = gain_a[0] + gain_a[1] + gain_a[2] + gain_a[3]
    for d in range(1, 4):
        to = dev(x_=lax.rem(xi + d, 4))
        send(remote(gain_b.at[xi], gain_b.at[xi], gb_ss.at[d - 1], gb_rs.at[d - 1], to))

    group(0)
    pass_on(2)
    beside(3)
    group(1)
    pass_on(3)
    group(2)
    group(3)

    for d in range(1, 4):
        src = gain_b.at[lax.rem(xi - d + 4, 4)]
        remote(src, src, gb_ss.at[d - 1], gb_rs.at[d - 1], partner).wait_recv()
    gains = gain_b[0] + gain_b[1] + gain_b[2] + gain_b[3]
    gk_out[...] = gains[0:1]
    gq_out[...] = gains[1:2]

    f_copy = remote(fs, fr, f_ss, f_rs, partner)

    @pl.when(active)
    def _():
        total = yred[3].astype(F32)
        for k in range(4):
            for j in range(1 if k == 3 else 0, 2):
                got_ = zin.at[k, j]
                remote(got_, got_, in_ss.at[k], in_rs.at[k, j], partner).wait_recv()
                total = total + got_[...].astype(F32)
        top, bottom = total[: ROWS // 2], total[ROWS // 2 :]
        fs[...] = jnp.where(first, bottom, top)
        f_copy.start()
        out_ref[...] = jnp.where(first, top, bottom).astype(BF16)
        f_copy.wait_send()

    @pl.when(jnp.logical_not(active))
    def _():
        f_copy.wait_recv()
        out_ref[...] = fr[...].astype(BF16)

    for when, copy in pending:
        if when is None:
            copy.wait_send()
        else:
            pl.when(when)(copy.wait_send)


def hand_over(a_ref, b_ref, c_ref, a_out, b_out, c_out, sems):
    copies = [
        pltpu.make_async_copy(src, dst, sems.at[i])
        for i, (src, dst) in enumerate([(a_ref, a_out), (b_ref, b_out), (c_ref, c_out)])
    ]
    for copy in copies:
        copy.start()
    for copy in copies:
        copy.wait()


def on_device(
    image_rows,
    key_weight,
    value_weight,
    key_gain,
    query_gain,
    queries,
    cotangent,
    text_doc,
    row_doc,
):
    width = image_rows.shape[2]
    half = width // 2
    quarter = half // 2
    tok = queries.shape[2]
    q_width = queries.shape[3]
    rows = row_doc.shape[1]
    vmem = pl.BlockSpec(memory_space=pltpu.VMEM)
    hbm = pl.BlockSpec(memory_space=pltpu.HBM)
    dma = pltpu.SemaphoreType.DMA
    stacked = tok * q_width // HEAD
    scratch = [
        pltpu.VMEM((8, width), BF16),
        pltpu.VMEM(key_gain.shape, F32),
        pltpu.VMEM(query_gain.shape, F32),
        pltpu.VMEM(text_doc.shape, jnp.int32),
        pltpu.VMEM(row_doc.shape, jnp.int32),
        pltpu.VMEM((half, 4 * HEAD), BF16),
        pltpu.VMEM((quarter, 4 * HEAD), BF16),
        pltpu.VMEM((stacked, HEAD), BF16),
        pltpu.VMEM((stacked, HEAD), BF16),
        pltpu.VMEM((stacked, HEAD), BF16),
        pltpu.VMEM((stacked, HEAD), F32),
        pltpu.VMEM((8, half), F32),
        pltpu.VMEM((8, half), F32),
        pltpu.VMEM((rows, stacked), F32),
        pltpu.VMEM((rows, stacked), F32),
        pltpu.VMEM((rows, stacked), BF16),
        pltpu.VMEM((8, stacked), F32),
        pltpu.VMEM((rows, HEAD), F32),
        pltpu.VMEM((rows, HEAD), F32),
        pltpu.VMEM((rows, HEAD), BF16),
        pltpu.VMEM((rows, half), BF16),
        pltpu.VMEM((rows, 2 * HEAD), F32),
        pltpu.VMEM((rows, 2 * HEAD), F32),
        pltpu.VMEM((rows, 2 * HEAD), F32),
        pltpu.VMEM((rows, 8 * HEAD), BF16),
        pltpu.VMEM((rows, quarter), BF16),
        pltpu.VMEM((2, 4, ROWS, quarter), BF16),
        pltpu.VMEM((2, 4, ROWS, quarter), BF16),
        pltpu.VMEM((2, 4, ROWS, quarter), BF16),
        pltpu.VMEM((4, ROWS, quarter), BF16),
        pltpu.VMEM((4, 2, ROWS, quarter), BF16),
        pltpu.VMEM((8, quarter), F32),
        pltpu.VMEM((8, quarter), F32),
        pltpu.VMEM((4, 8, HEAD), F32),
        pltpu.VMEM((4, 8, HEAD), F32),
        pltpu.VMEM((rows, 2 * tok), F32),
        dma((5,)), dma((2,)), dma((2,)), dma((2,)),
        dma((4,)), dma((4,)), dma((2, 2)), dma((2, 2)), dma((2,)), dma((2,)),
        dma((2, q_width // HEAD)), dma, dma,
        dma((3, 2)), dma((2, 2)), dma((4, 2)),
        dma((4, 2, 2)), dma((4, 2, 2)), dma((4, 2)), dma((4, 2)),
        dma((4,)), dma((4,)), dma((4, 3)), dma((4, 3)),
        dma((2, 4)), dma((2, 4)), dma((2, 4)), dma((2, 4)), dma((2, 4)), dma((2, 4)),
        dma((4,)), dma((4, 2)), dma, dma,
        dma((3,)), dma((3,)), dma((3,)), dma((3,)),
    ]
    grad, gain_key, gain_query = pl.pallas_call(
        kernel,
        name="image_row_gradients",
        out_shape=(
            jax.ShapeDtypeStruct((8, quarter), BF16),
            jax.ShapeDtypeStruct((1, HEAD), F32),
            jax.ShapeDtypeStruct((1, HEAD), F32),
        ),
        in_specs=[hbm] * 9,
        out_specs=(vmem, vmem, vmem),
        scratch_shapes=scratch,
        compiler_params=pltpu.CompilerParams(
            collective_id=0, has_side_effects=True, vmem_limit_bytes=62 * 1024 * 1024
        ),
    )(
        image_rows[0], key_weight[0], value_weight[0], key_gain, query_gain,
        queries[0, 0], cotangent[0, 0], text_doc, row_doc,
    )
    anywhere = pl.BlockSpec(memory_space=pl.ANY)
    return pl.pallas_call(
        hand_over,
        name="hand_over",
        out_shape=(
            jax.ShapeDtypeStruct((1, 8, quarter), BF16),
            jax.ShapeDtypeStruct((1, HEAD), F32),
            jax.ShapeDtypeStruct((1, HEAD), F32),
        ),
        in_specs=[anywhere] * 3,
        out_specs=(anywhere,) * 3,
        scratch_shapes=[dma((3,))],
        compiler_params=pltpu.CompilerParams(vmem_limit_bytes=62 * 1024 * 1024),
    )(grad[None], gain_key, gain_query)


def solution(mesh):
    in_specs = (
        P("dp", "section", None),
        P("section", None, "tensor"),
        P("section", None, "tensor"),
        P(),
        P(),
        P("dp", "section", None, "tensor"),
        P("dp", "section", None, "tensor"),
        P("dp", None),
        P("dp", None),
    )
    out_specs = (P("dp", "section", "tensor"), P("section", None), P("section", None))
    return jax.shard_map(
        on_device, mesh=mesh, in_specs=in_specs, out_specs=out_specs, check_vma=False
    )
```
